256 devices in a mesh: dp: 16 (over y, z_lo), tensor: 16 (over z_hi, x, core).
Axes of the slice: x: 4, y: 4, z: 8 (z_hi: 2, z_lo: 4; z = z_hi * 4 + z_lo), core: 2. Of those that a mesh axis runs over, the one named last changes fastest.
Arguments:
- activations: bfloat16 [2048, 8192], P('dp', 'tensor'), may hold values from -6 to 6
- out_grads: bfloat16 [2048, 28672], P('dp', 'tensor'), may hold values from -12 to 12
- basis_in: bfloat16 [8192, 8192], P('dp', 'tensor'), may hold values from -0.0625 to 0.0625
- basis_out: bfloat16 [28672, 14336], P('tensor', 'dp'), may hold values from -0.03125 to 0.03125
Outputs:
- correction: float32 [8192, 14336], P('tensor', 'dp')
The draws below stay inside these ranges and needn't reach their ends.
All inputs are finite; a program needn't handle non-finite values.
Results may differ from the reference program's by a relative error of at most 0.0033.
Values may be sent and summed in bfloat16 or wider, within the bound.
A program may use at most 128 MiB of HBM per device.

```python
import math
import jax
import jax.numpy as jnp
from jax import lax

D = 8192
FF = 28672
JW = 14336
SEQ = 128
EXAMPLES = 16
TOKENS = 2048


def draw_out_grads(key, part):
    key = jax.random.fold_in(key, 11)
    scale_key, noise_key = jax.random.split(key, 2)
    groups = TOKENS // SEQ
    scales = jnp.exp(jax.random.uniform(scale_key, (groups, 1, 1), jnp.float32, math.log(0.3), math.log(3.0)))
    noise_part = jnp.clip(jax.random.normal(noise_key, (groups, SEQ, FF), jnp.float32), -4.0, 4.0)
    values = scales * noise_part
    return values.reshape(TOKENS, FF).astype(jnp.bfloat16)


def level_of(key, shape, shards, low, top_value):
    def one(dim, blocks):
        heights = jax.random.uniform(jax.random.fold_in(jax.random.fold_in(key, 6), dim), (blocks,), jnp.float32, low / len(shards), top_value / len(shards))
        return jnp.repeat(jnp.exp(heights), shape[dim] // blocks).reshape((-1,) + (1,) * (len(shape) - dim - 1))

    loudness = one(*shards[0])
    for cut in shards[1:]:
        loudness = loudness * one(*cut)
    return loudness


def normal_values(stream_key, shape, scale, bound, shards=(), kind=jnp.bfloat16):
    gain = level_of(stream_key, shape, shards, -0.22, 0.18) if shards else 1.0
    result = jax.random.normal(stream_key, shape, jnp.float32) * scale * gain
    return jnp.minimum(jnp.maximum(result, -bound), bound).astype(kind)


def setup_inputs(seed: int = 0) -> dict:
    key_list = jax.random.split(jax.random.key(seed), 5)
    activations = normal_values(key_list[0], (TOKENS, D), 1.0, 6.0, ((0, 16), (1, 16)))
    out_grads = draw_out_grads(jax.random.fold_in(key_list[4], 71), 0)
    basis_in = normal_values(key_list[2], (D, D), D ** -0.5, 0.0625, ((0, 16), (1, 16)))
    basis_out = normal_values(key_list[3], (FF, JW), FF ** -0.5, 0.03125, ((0, 16), (1, 16)))
    return {"activations": activations, "out_grads": out_grads, "basis_in": basis_in, "basis_out": basis_out}


def reference(activations, out_grads, basis_in, basis_out):
    act_rot = jnp.dot(activations, basis_in, preferred_element_type=jnp.float32).astype(jnp.bfloat16)
    grad_rot = jnp.dot(out_grads, basis_out, preferred_element_type=jnp.float32).astype(jnp.bfloat16)
    act_examples = act_rot.reshape(EXAMPLES, SEQ, D)
    grad_examples = grad_rot.reshape(EXAMPLES, SEQ, JW)

    def add_example(position, running):
        left_rows = lax.dynamic_index_in_dim(act_examples, position, 0, keepdims=False)
        right_rows = lax.dynamic_index_in_dim(grad_examples, position, 0, keepdims=False)
        product = jnp.dot(left_rows.T, right_rows, preferred_element_type=jnp.float32)
        return running + product * product

    start_sum = jnp.zeros((D, JW), jnp.float32)
    running = lax.fori_loop(0, EXAMPLES, add_example, start_sum)
    return running / (EXAMPLES * SEQ)
```

```python
import functools

import jax
import jax.numpy as jnp
from jax import lax
from jax.experimental import pallas as pl
from jax.experimental.pallas import tpu as pltpu
from jax.sharding import PartitionSpec as P

MESH = pl.DeviceIdType.MESH
F32 = jnp.float32
BF16 = jnp.bfloat16
SEQ = 128


class Copies:
    def __init__(self, send_sems):
        self.send_sems = send_sems
        self.sent = []

    def send(self, src, dst, recv_sem, to, cond=None):
        index = len(self.sent)

        def build():
            return pltpu.make_async_remote_copy(
                src_ref=src,
                dst_ref=dst,
                send_sem=self.send_sems.at[index],
                recv_sem=recv_sem,
                device_id=to,
                device_id_type=MESH,
            )

        if cond is None:
            build().start()
        else:
            pl.when(cond)(lambda: build().start())
        self.sent.append((build, cond))

    def finish(self):
        for build, cond in self.sent:
            if cond is None:
                build().wait_send()
            else:
                pl.when(cond)(lambda build=build: build().wait_send())


def kernel(
    tokens_ref, grads_ref, bin_ref, bout_ref, out_ref,
    a_all, part, core_in, x_in, x_sum, z_in, grad, b1, a1, r_part, r_in, rt,
    send_sems, local_sems, a_sem, a_half_sem, b1_sem, b1_half_sem, a1_first_sem, a1_x_sem, a1_core_sem,
    r_sem, rt_z_sem, rt_y_sem, rt_half_sem, core_sem, x_sem, z_sem, gz_sem, gx_sem, gc_sem,
):
    dp, tensor = lax.axis_index("dp"), lax.axis_index("tensor")
    y, zl = dp // 4, dp % 4
    zh, x, c = tensor // 8, (tensor // 2) % 4, tensor % 2

    def dev(x=x, y=y, zl=zl, zh=zh, c=c):
        return (y * 4 + zl, zh * 8 + x * 2 + c)

    def ring(v, k):
        return lax.rem(v + k + 4, 4)

    up_y, down_y = dev(y=ring(y, 1)), dev(y=ring(y, -1))
    core_mate, z_mate = dev(c=1 - c), dev(zh=1 - zh)
    x_others = [dev(x=ring(x, k)) for k in (1, 2, 3)]
    copies = Copies(send_sems)

    barrier = pltpu.get_barrier_semaphore()
    greeted = 0
    for dz in range(4):
        for dh in range(2):
            for dc in range(2):
                if dz or dh or dc:
                    pl.semaphore_signal(
                        barrier, inc=1, device_id=dev(zl=ring(zl, dz), zh=(zh + dh) % 2, c=(c + dc) % 2), device_id_type=MESH
                    )
                    greeted += 1
    for other in [up_y, down_y] + x_others:
        pl.semaphore_signal(barrier, inc=1, device_id=other, device_id_type=MESH)
        greeted += 1
    pl.semaphore_wait(barrier, greeted)

    def got(ref, sem):
        pltpu.make_async_copy(ref, ref, sem).wait()

    def shard(yy, zz):
        return a_all.at[pl.ds(pl.multiple_of((yy * 4 + zz) * SEQ, SEQ), SEQ)]

    def half_shard(yy, zz, half):
        return a_all.at[pl.ds(pl.multiple_of((yy * 4 + zz) * SEQ + half * (SEQ // 2), SEQ // 2), SEQ // 2)]

    def send_shard_y(zz, src, cond=None):
        copies.send(src, shard(y, zz), a_sem.at[1, zz], up_y, cond)
        copies.send(src, shard(y, zz), a_sem.at[2, zz], down_y, cond)

    low, high, opposite = ring(y, -1), ring(y, 1), ring(y, 2)

    def relay_shard_y(zz, cond=None):
        def await_both():
            got(shard(low, zz), a_sem.at[1, zz])
            got(shard(high, zz), a_sem.at[2, zz])

        await_both() if cond is None else pl.when(cond)(await_both)
        copies.send(half_shard(low, zz, 0), half_shard(low, zz, 0), a_half_sem.at[0, zz], up_y, cond)
        copies.send(half_shard(high, zz, 1), half_shard(high, zz, 1), a_half_sem.at[1, zz], down_y, cond)

    def relay_step(k):
        for sign in (-1, 1):
            source = zl + sign * k
            relay_shard_y(jnp.clip(source, 0, 3), jnp.logical_and(source >= 0, source <= 3))

    copies.send(grads_ref, shard(y, zl), a_sem.at[0, zl], dev(zl=jnp.minimum(zl + 1, 3)), zl < 3)
    copies.send(grads_ref, shard(y, zl), a_sem.at[0, zl], dev(zl=jnp.maximum(zl - 1, 0)), zl > 0)

    z_target = 2 * (x % 2) + c
    a1_block = a1.at[zl % 2, 2 * zh + x // 2, zl // 2]
    for h in range(2):
        mine = jnp.logical_and(zl == z_target, zh == h)
        copies.send(
            tokens_ref, a1_block, a1_first_sem.at[zl // 2, zh], dev(zl=z_target, zh=h, c=zl % 2), jnp.logical_not(mine)
        )

        @pl.when(mine)
        def _():
            own = pltpu.make_async_copy(tokens_ref, a1_block, local_sems.at[2])
            own.start()
            own.wait()

    send_shard_y(zl, grads_ref)

    def b1_block(yy):
        return b1.at[pl.ds(pl.multiple_of(yy * 512, 512), 512)]

    def b1_half(yy, half):
        return b1.at[pl.ds(pl.multiple_of(yy * 512 + half * 256, 256), 256)]

    copies.send(bin_ref, b1_block(y), b1_sem.at[0], up_y)
    copies.send(bin_ref, b1_block(y), b1_sem.at[1], down_y)
    own_a = pltpu.make_async_copy(grads_ref, shard(y, zl), local_sems.at[0])
    own_b = pltpu.make_async_copy(bin_ref, b1_block(y), local_sems.at[1])
    own_a.start()
    own_b.start()

    def z_step(k):
        for sign in (-1, 1):
            source = zl + sign * k
            there = jnp.logical_and(source >= 0, source <= 3)
            zz = jnp.clip(source, 0, 3)
            pl.when(there)(lambda zz=zz: got(shard(y, zz), a_sem.at[0, zz]))
            if k < 3:
                onward = zl - sign
                copies.send(
                    shard(y, zz), shard(y, zz), a_sem.at[0, zz], dev(zl=jnp.clip(onward, 0, 3)),
                    jnp.logical_and(there, jnp.logical_and(onward >= 0, onward <= 3)),
                )
            send_shard_y(zz, shard(y, zz), there)

    z_step(1)

    parity = zl // 2
    holds = x % 2 == parity
    for zhalf in range(2):
        for h in range(2):
            mine = jnp.logical_and(c + 2 * zhalf == zl, zh == h)
            pl.when(jnp.logical_and(holds, jnp.logical_not(mine)))(
                lambda zhalf=zhalf, h=h: got(a1.at[c, 2 * h + x // 2, zhalf], a1_first_sem.at[zhalf, h])
            )
    for h in range(2):
        block = a1.at[c, 2 * h + x // 2]
        for other in x_others:
            copies.send(block, block, a1_x_sem.at[2 * h + x // 2], other, holds)

    relay_shard_y(zl)

    got(b1_block(low), b1_sem.at[0])
    copies.send(b1_half(low, 0), b1_half(low, 0), b1_half_sem.at[0], up_y)
    got(b1_block(high), b1_sem.at[1])
    copies.send(b1_half(high, 1), b1_half(high, 1), b1_half_sem.at[1], down_y)

    for kq in range(4):
        pl.when(parity + 2 * (kq % 2) != x)(lambda kq=kq: got(a1.at[c, kq], a1_x_sem.at[kq]))
    copies.send(a1.at[c], a1.at[c], a1_core_sem.at[0], core_mate)

    z_step(2)
    relay_step(1)
    z_step(3)
    own_a.wait()

    half_rows, x_rows, z_rows = 256, 64, 32

    def rotate(g):
        @pl.loop(0, 2)
        def _(m):
            rows = pl.ds(pl.multiple_of(g * 512 + m * 256, 256), 256)
            part[rows, :] = jnp.dot(a_all[rows, :], bout_ref[...], preferred_element_type=F32)

        theirs = part.at[pl.ds(pl.multiple_of(g * 512 + (1 - c) * 256, 256), 256)]
        copies.send(theirs, core_in.at[g], core_sem.at[g], core_mate)

    def sum_core(g):
        got(core_in.at[g], core_sem.at[g])
        base = g * 512 + c * 256
        rows = pl.ds(pl.multiple_of(base, 256), 256)
        part[rows, :] = part[rows, :] + core_in[g]
        for k, other in zip((1, 2, 3), x_others):
            piece = part.at[pl.ds(pl.multiple_of(base + ring(x, k) * x_rows, x_rows), x_rows)]
            copies.send(piece, x_in.at[g, k - 1], x_sem.at[g, k - 1], other)

    def sum_x(g):
        for k in range(3):
            got(x_in.at[g, k], x_sem.at[g, k])
        rows = pl.ds(pl.multiple_of(g * 512 + c * 256 + x * x_rows, x_rows), x_rows)
        x_sum[g] = ((part[rows, :] + x_in[g, 0]) + (x_in[g, 1] + x_in[g, 2])).reshape(2, z_rows, x_sum.shape[3])
        copies.send(x_sum.at[g, 1 - zh], z_in.at[g], z_sem.at[g], z_mate)

    def grad_rows(g, first, count):
        return grad.at[pl.ds(pl.multiple_of(g * 512 + first, count), count)]

    def sum_z(g):
        got(z_in.at[g], z_sem.at[g])
        first = c * 256 + x * x_rows + zh * z_rows
        rows = pl.ds(pl.multiple_of(g * 512 + first, z_rows), z_rows)
        grad[rows, :] = (x_sum[g, zh] + z_in[g]).astype(BF16)
        own = grad_rows(g, first, z_rows)
        copies.send(own, own, gz_sem.at[g], z_mate)

    def spread_x(g):
        got(grad_rows(g, c * 256 + x * x_rows + (1 - zh) * z_rows, z_rows), gz_sem.at[g])
        own = grad_rows(g, c * 256 + x * x_rows, x_rows)
        for k, other in zip((1, 2, 3), x_others):
            copies.send(own, own, gx_sem.at[g, k - 1], other)

    def spread_core(g):
        for k in (1, 2, 3):
            got(grad_rows(g, c * 256 + ring(x, -k) * x_rows, x_rows), gx_sem.at[g, k - 1])
        own = grad_rows(g, c * 256, half_rows)
        copies.send(own, own, gc_sem.at[g], core_mate)

    def fit(g, first):
        got(grad_rows(g, (1 - c) * 256, half_rows), gc_sem.at[g])

        @pl.loop(0, 7)
        def _(j):
            cols = pl.ds(pl.multiple_of(j * 128, 128), 128)
            total = None
            for n in range(4):
                right = grad[pl.ds(pl.multiple_of(g * 512 + n * SEQ, SEQ), SEQ), cols]
                product = jnp.dot(rt[g * 4 + n], right, preferred_element_type=F32)
                square = product * product
                total = square if total is None else total + square
            total = total * (1.0 / 2048)
            out_ref[:, cols] = total if first else out_ref[:, cols] + total

    own_b.wait()
    got(b1_half(opposite, 0), b1_half_sem.at[0])
    got(b1_half(opposite, 1), b1_half_sem.at[1])
    got(a1.at[1 - c], a1_core_sem.at[0])

    @pl.loop(0, 4)
    def _(kq):
        left = a1[:, kq].reshape(512, 512)
        right = b1[pl.ds(pl.multiple_of(kq * 512, 512), 512), :]
        term = jnp.dot(left, right, preferred_element_type=F32)

        @pl.when(kq == 0)
        def _():
            r_part[...] = term.reshape(4, SEQ, 512)

        @pl.when(kq != 0)
        def _():
            r_part[...] += term.reshape(4, SEQ, 512)

    def place(zz):
        return (zz % 2) * 2 + zz // 2

    for k in (1, 2, 3):
        zz = ring(zl, k)
        copies.send(r_part.at[place(zz)], r_in.at[k - 1], r_sem.at[k - 1], dev(zl=zz))

    rotate(y)
    relay_step(2)
    relay_step(3)

    def r_block(yy, zz):
        return rt.at[yy * 4 + zz]

    def r_half(yy, zz, half):
        return rt.at[yy * 4 + zz, pl.ds(half * 256, 256)]

    def send_r_y(zz):
        copies.send(r_block(y, zz), r_block(y, zz), rt_y_sem.at[0, zz], up_y)
        copies.send(r_block(y, zz), r_block(y, zz), rt_y_sem.at[1, zz], down_y)

    for k in range(3):
        got(r_in.at[k], r_sem.at[k])
    own_r = (r_part[place(zl)] + r_in[0]) + (r_in[1] + r_in[2])
    rt[y * 4 + zl] = own_r.T.astype(BF16)
    for k in (1, 2, 3):
        copies.send(r_block(y, zl), r_block(y, zl), rt_z_sem.at[k - 1], dev(zl=ring(zl, k)))
    send_r_y(zl)
    sum_core(y)

    for k in (1, 2, 3):
        zz = ring(zl, -k)
        got(r_block(y, zz), rt_z_sem.at[k - 1])
        send_r_y(zz)
    sum_x(y)

    def await_group(yy, which):
        for k in range(4):
            if which == 3:
                got(half_shard(yy, k, 0), a_half_sem.at[0, k])
                got(half_shard(yy, k, 1), a_half_sem.at[1, k])

    rotate(high)
    sum_z(y)
    rotate(low)
    spread_x(y)
    sum_core(high)
    sum_core(low)
    spread_core(y)

    for k in range(4):
        zz = ring(zl, k)
        got(r_block(low, zz), rt_y_sem.at[0, zz])
        copies.send(r_half(low, zz, 0), r_half(low, zz, 0), rt_half_sem.at[0, zz], up_y)
        got(r_block(high, zz), rt_y_sem.at[1, zz])
        copies.send(r_half(high, zz, 1), r_half(high, zz, 1), rt_half_sem.at[1, zz], down_y)

    sum_x(high)
    sum_x(low)
    await_group(opposite, 3)
    rotate(opposite)
    sum_z(high)
    sum_z(low)
    sum_core(opposite)
    spread_x(high)
    spread_x(low)
    fit(y, True)
    sum_x(opposite)
    spread_core(high)
    spread_core(low)
    sum_z(opposite)
    fit(high, False)
    spread_x(opposite)
    fit(low, False)
    spread_core(opposite)
    for k in range(4):
        got(r_half(opposite, k, 0), rt_half_sem.at[0, k])
        got(r_half(opposite, k, 1), rt_half_sem.at[1, k])
    fit(opposite, False)
    copies.finish()


def local(activations, out_grads, basis_in, basis_out):
    vmem = pl.BlockSpec(memory_space=pltpu.VMEM)
    dma = pltpu.SemaphoreType.DMA
    return pl.pallas_call(
        kernel,
        out_shape=jax.ShapeDtypeStruct((512, 896), F32),
        in_specs=[vmem] * 4,
        out_specs=vmem,
        scratch_shapes=[
            pltpu.VMEM((2048, 1792), BF16),
            pltpu.VMEM((2048, 896), F32),
            pltpu.VMEM((4, 256, 896), F32),
            pltpu.VMEM((4, 3, 64, 896), F32),
            pltpu.VMEM((4, 2, 32, 896), F32),
            pltpu.VMEM((4, 32, 896), F32),
            pltpu.VMEM((2048, 896), BF16),
            pltpu.VMEM((2048, 512), BF16),
            pltpu.VMEM((2, 4, 2, 128, 512), BF16),
            pltpu.VMEM((4, 128, 512), F32),
            pltpu.VMEM((3, 128, 512), F32),
            pltpu.VMEM((16, 512, 128), BF16),
            dma((160,)),
            dma((3,)),
            dma((3, 4)),
            dma((2, 4)),
            dma((2,)),
            dma((2,)),
            dma((2, 2)),
            dma((4,)),
            dma((1,)),
            dma((3,)),
            dma((3,)),
            dma((2, 4)),
            dma((2, 4)),
            dma((4,)),
            dma((4, 3)),
            dma((4,)),
            dma((4,)),
            dma((4, 3)),
            dma((4,)),
        ],
        compiler_params=pltpu.CompilerParams(
            collective_id=0, has_side_effects=True, vmem_limit_bytes=56 * 2**20
        ),
        cost_estimate=pl.CostEstimate(flops=9_600_000_000, bytes_accessed=6_000_000, transcendentals=0),
    )(activations, out_grads, basis_in, basis_out)


def solution(mesh):
    in_specs = (P("dp", "tensor"), P("dp", "tensor"), P("dp", "tensor"), P("tensor", "dp"))
    out_specs = P("tensor", "dp")
    return jax.shard_map(local, mesh=mesh, in_specs=in_specs, out_specs=out_specs, check_vma=False)
```

```python
import functools

import jax
import jax.numpy as jnp
from jax import lax
from jax.experimental import pallas as pl
from jax.experimental.pallas import tpu as pltpu
from jax.sharding import PartitionSpec as P

MESH = pl.DeviceIdType.MESH
F32 = jnp.float32
BF16 = jnp.bfloat16
SEQ = 128


class Copies:
    def __init__(self, send_sems):
        self.send_sems = send_sems
        self.sent = []

    def send(self, src, dst, recv_sem, to, cond=None):
        index = len(self.sent)

        def build():
            return pltpu.make_async_remote_copy(
                src_ref=src,
                dst_ref=dst,
                send_sem=self.send_sems.at[index],
                recv_sem=recv_sem,
                device_id=to,
                device_id_type=MESH,
            )

        if cond is None:
            build().start()
        else:
            pl.when(cond)(lambda: build().start())
        self.sent.append((build, cond))

    def finish(self):
        for build, cond in self.sent:
            if cond is None:
                build().wait_send()
            else:
                pl.when(cond)(lambda build=build: build().wait_send())


def kernel(
    x_type, r_type,
    tokens_ref, grads_ref, bin_ref, bout_ref, out_ref,
    a_all, part, core_in, x_out, x_in, x_sum, z_in, grad, b1, a1, r_part, r_out, r_in, rt,
    send_sems, local_sems, a_sem, a_half_sem, b1_sem, b1_half_sem, a1_first_sem, a1_x_sem, a1_core_sem,
    r_sem, rt_z_sem, rt_y_sem, rt_half_sem, core_sem, x_sem, z_sem, gz_sem, gx_sem, gc_sem,
):
    dp, tensor = lax.axis_index("dp"), lax.axis_index("tensor")
    y, zl = dp // 4, dp % 4
    zh, x, c = tensor // 8, (tensor // 2) % 4, tensor % 2

    def dev(x=x, y=y, zl=zl, zh=zh, c=c):
        return (y * 4 + zl, zh * 8 + x * 2 + c)

    def ring(v, k):
        return lax.rem(v + k + 4, 4)

    up_y, down_y = dev(y=ring(y, 1)), dev(y=ring(y, -1))
    core_mate, z_mate = dev(c=1 - c), dev(zh=1 - zh)
    x_others = [dev(x=ring(x, k)) for k in (1, 2, 3)]
    copies = Copies(send_sems)

    barrier = pltpu.get_barrier_semaphore()
    greeted = 0
    for dz in range(4):
        for dh in range(2):
            for dc in range(2):
                if dz or dh or dc:
                    pl.semaphore_signal(
                        barrier, inc=1, device_id=dev(zl=ring(zl, dz), zh=(zh + dh) % 2, c=(c + dc) % 2), device_id_type=MESH
                    )
                    greeted += 1
    for other in [up_y, down_y] + x_others:
        pl.semaphore_signal(barrier, inc=1, device_id=other, device_id_type=MESH)
        greeted += 1
    pl.semaphore_wait(barrier, greeted)

    def got(ref, sem):
        pltpu.make_async_copy(ref, ref, sem).wait()

    def shard(yy, zz):
        return a_all.at[pl.ds(pl.multiple_of((yy * 4 + zz) * SEQ, SEQ), SEQ)]

    def half_shard(yy, zz, half):
        return a_all.at[pl.ds(pl.multiple_of((yy * 4 + zz) * SEQ + half * (SEQ // 2), SEQ // 2), SEQ // 2)]

    def send_shard_y(zz, src, cond=None):
        copies.send(src, shard(y, zz), a_sem.at[1, zz], up_y, cond)
        copies.send(src, shard(y, zz), a_sem.at[2, zz], down_y, cond)

    low, high, opposite = ring(y, -1), ring(y, 1), ring(y, 2)

    def relay_shard_y(zz):
        got(shard(low, zz), a_sem.at[1, zz])
        copies.send(half_shard(low, zz, 0), half_shard(low, zz, 0), a_half_sem.at[0, zz], up_y)
        got(shard(high, zz), a_sem.at[2, zz])
        copies.send(half_shard(high, zz, 1), half_shard(high, zz, 1), a_half_sem.at[1, zz], down_y)

    z_target = 2 * (x % 2) + c
    a1_block = a1.at[zl % 2, 2 * zh + x // 2, zl // 2]
    for h in range(2):
        mine = jnp.logical_and(zl == z_target, zh == h)
        copies.send(
            tokens_ref, a1_block, a1_first_sem.at[zl // 2, zh], dev(zl=z_target, zh=h, c=zl % 2), jnp.logical_not(mine)
        )

        @pl.when(mine)
        def _():
            own = pltpu.make_async_copy(tokens_ref, a1_block, local_sems.at[2])
            own.start()
            own.wait()

    def b1_block(yy):
        return b1.at[pl.ds(pl.multiple_of(yy * 512, 512), 512)]

    def b1_half(yy, half):
        return b1.at[pl.ds(pl.multiple_of(yy * 512 + half * 256, 256), 256)]

    copies.send(bin_ref, b1_block(y), b1_sem.at[0], up_y)
    copies.send(bin_ref, b1_block(y), b1_sem.at[1], down_y)
    copies.send(grads_ref, shard(y, zl), a_sem.at[0, zl], dev(zl=jnp.minimum(zl + 1, 3)), zl < 3)
    copies.send(grads_ref, shard(y, zl), a_sem.at[0, zl], dev(zl=jnp.maximum(zl - 1, 0)), zl > 0)

    own_a = pltpu.make_async_copy(grads_ref, shard(y, zl), local_sems.at[0])
    own_b = pltpu.make_async_copy(bin_ref, b1_block(y), local_sems.at[1])
    own_a.start()
    own_b.start()

    def z_step(k):
        for sign in (-1, 1):
            source = zl + sign * k
            there = jnp.logical_and(source >= 0, source <= 3)
            zz = jnp.clip(source, 0, 3)
            pl.when(there)(lambda zz=zz: got(shard(y, zz), a_sem.at[0, zz]))
            if k < 3:
                onward = zl - sign
                copies.send(
                    shard(y, zz), shard(y, zz), a_sem.at[0, zz], dev(zl=jnp.clip(onward, 0, 3)),
                    jnp.logical_and(there, jnp.logical_and(onward >= 0, onward <= 3)),
                )
            send_shard_y(zz, shard(y, zz), there)

    parity = zl // 2

    def tokens_x():
        holds = x % 2 == parity
        for zhalf in range(2):
            for h in range(2):
                mine = jnp.logical_and(c + 2 * zhalf == zl, zh == h)
                pl.when(jnp.logical_and(holds, jnp.logical_not(mine)))(
                    lambda zhalf=zhalf, h=h: got(a1.at[c, 2 * h + x // 2, zhalf], a1_first_sem.at[zhalf, h])
                )
        for h in range(2):
            block = a1.at[c, 2 * h + x // 2]
            for other in x_others:
                copies.send(block, block, a1_x_sem.at[2 * h + x // 2], other, holds)

    def tokens_core():
        for kq in range(4):
            pl.when(parity + 2 * (kq % 2) != x)(lambda kq=kq: got(a1.at[c, kq], a1_x_sem.at[kq]))
        copies.send(a1.at[c], a1.at[c], a1_core_sem.at[0], core_mate)

    def basis_relay():
        got(b1_block(low), b1_sem.at[0])
        copies.send(b1_half(low, 0), b1_half(low, 0), b1_half_sem.at[0], up_y)
        got(b1_block(high), b1_sem.at[1])
        copies.send(b1_half(high, 1), b1_half(high, 1), b1_half_sem.at[1], down_y)

    near, far = zl // 2, 1 - zl // 2
    units = [(y, near), (y, far), (high, near), (low, near), (high, far), (low, far), (opposite, near), (opposite, far)]

    def rotate(i):
        g, h = units[i]
        rows = pl.ds(pl.multiple_of(g * 512 + h * 256, 256), 256)
        part[i] = jnp.dot(a_all[rows, :], bout_ref[...], preferred_element_type=F32)
        theirs = part.at[i, pl.ds(pl.multiple_of((1 - c) * 128, 128), 128)]
        copies.send(theirs, core_in.at[i], core_sem.at[i], core_mate)

    def sum_core(i):
        got(core_in.at[i], core_sem.at[i])
        rows = pl.ds(pl.multiple_of(c * 128, 128), 128)
        chip = part[i, rows, :] + core_in[i]
        part[i, rows, :] = chip
        if x_type == F32:
            for k, other in zip((1, 2, 3), x_others):
                piece = part.at[i, pl.ds(pl.multiple_of(c * 128 + ring(x, k) * 32, 32), 32)]
                copies.send(piece, x_in.at[i, k - 1], x_sem.at[i, k - 1], other)
        else:
            x_out[i] = chip.astype(x_type).reshape(4, 32, chip.shape[1])
            for k, other in zip((1, 2, 3), x_others):
                copies.send(x_out.at[i, ring(x, k)], x_in.at[i, k - 1], x_sem.at[i, k - 1], other)

    def sum_x(i):
        for k in range(3):
            got(x_in.at[i, k], x_sem.at[i, k])
        rows = pl.ds(pl.multiple_of(c * 128 + x * 32, 32), 32)
        others = [x_in[i, k].astype(F32) for k in range(3)]
        x_sum[i] = ((part[i, rows, :] + others[0]) + (others[1] + others[2])).reshape(2, 16, part.shape[2])
        copies.send(x_sum.at[i, 1 - zh], z_in.at[i], z_sem.at[i], z_mate)

    def grad_rows(i, first, count):
        return grad.at[i, pl.ds(pl.multiple_of(first, count), count)]

    def sum_z(i):
        got(z_in.at[i], z_sem.at[i])
        first = c * 128 + x * 32 + zh * 16
        grad[i, pl.ds(pl.multiple_of(first, 16), 16), :] = (x_sum[i, zh] + z_in[i]).astype(BF16)
        own = grad_rows(i, first, 16)
        copies.send(own, own, gz_sem.at[i], z_mate)

    def spread_x(i):
        got(grad_rows(i, c * 128 + x * 32 + (1 - zh) * 16, 16), gz_sem.at[i])
        own = grad_rows(i, c * 128 + x * 32, 32)
        for k, other in zip((1, 2, 3), x_others):
            copies.send(own, own, gx_sem.at[i, k - 1], other)

    def spread_core(i):
        for k in (1, 2, 3):
            got(grad_rows(i, c * 128 + ring(x, -k) * 32, 32), gx_sem.at[i, k - 1])
        own = grad_rows(i, c * 128, 128)
        copies.send(own, own, gc_sem.at[i], core_mate)

    def fit(i):
        got(grad_rows(i, (1 - c) * 128, 128), gc_sem.at[i])
        g, h = units[i]

        @pl.loop(0, 7)
        def _(j):
            cols = pl.ds(pl.multiple_of(j * 128, 128), 128)
            total = None
            for n in range(2):
                right = grad[i, n * SEQ:(n + 1) * SEQ, cols]
                product = jnp.dot(rt[g * 4 + h * 2 + n], right, preferred_element_type=F32)
                square = product * product
                total = square if total is None else total + square
            total = total * (1.0 / 2048)
            out_ref[:, cols] = total if i == 0 else out_ref[:, cols] + total

    def place(zz):
        return (zz % 2) * 2 + zz // 2

    def rotate_act():
        own_b.wait()
        got(b1_half(opposite, 0), b1_half_sem.at[0])
        got(b1_half(opposite, 1), b1_half_sem.at[1])
        got(a1.at[1 - c], a1_core_sem.at[0])

        @pl.loop(0, 4)
        def _(kq):
            left = a1[:, kq].reshape(512, 512)
            right = b1[pl.ds(pl.multiple_of(kq * 512, 512), 512), :]
            term = jnp.dot(left, right, preferred_element_type=F32)

            @pl.when(kq == 0)
            def _():
                r_part[...] = term.reshape(4, SEQ, 512)

            @pl.when(kq != 0)
            def _():
                r_part[...] += term.reshape(4, SEQ, 512)

        source = r_part
        if r_type != F32:
            r_out[...] = r_part[...].astype(r_type)
            source = r_out
        for k in (1, 2, 3):
            zz = ring(zl, k)
            copies.send(source.at[place(zz)], r_in.at[k - 1], r_sem.at[k - 1], dev(zl=zz))

    def r_block(yy, zz):
        return rt.at[yy * 4 + zz]

    def r_half(yy, zz, half):
        return rt.at[yy * 4 + zz, pl.ds(half * 256, 256)]

    def send_r_y(zz):
        copies.send(r_block(y, zz), r_block(y, zz), rt_y_sem.at[0, zz], up_y)
        copies.send(r_block(y, zz), r_block(y, zz), rt_y_sem.at[1, zz], down_y)

    def sum_act():
        for k in range(3):
            got(r_in.at[k], r_sem.at[k])
        others = [r_in[k].astype(F32) for k in range(3)]
        own_r = (r_part[place(zl)] + others[0]) + (others[1] + others[2])
        rt[y * 4 + zl] = own_r.T.astype(BF16)
        for k in (1, 2, 3):
            copies.send(r_block(y, zl), r_block(y, zl), rt_z_sem.at[k - 1], dev(zl=ring(zl, k)))
        send_r_y(zl)

    def act_y(k):
        zz = ring(zl, -k)
        got(r_block(y, zz), rt_z_sem.at[k - 1])
        send_r_y(zz)

    def act_relay(k):
        zz = ring(zl, -k)
        got(r_block(low, zz), rt_y_sem.at[0, zz])
        copies.send(r_half(low, zz, 0), r_half(low, zz, 0), rt_half_sem.at[0, zz], up_y)
        got(r_block(high, zz), rt_y_sem.at[1, zz])
        copies.send(r_half(high, zz, 1), r_half(high, zz, 1), rt_half_sem.at[1, zz], down_y)

    def act_opposite():
        for k in range(4):
            got(r_half(opposite, k, 0), rt_half_sem.at[0, k])
            got(r_half(opposite, k, 1), rt_half_sem.at[1, k])

    def opposite_pair(h):
        for k in range(2):
            got(half_shard(opposite, 2 * h + k, 0), a_half_sem.at[0, 2 * h + k])
            got(half_shard(opposite, 2 * h + k, 1), a_half_sem.at[1, 2 * h + k])

    mate = zl + 1 - 2 * (zl % 2)

    def relay_far():
        relay_shard_y(2 * far)
        relay_shard_y(2 * far + 1)

    stages = [rotate, sum_core, sum_x, sum_z, spread_x, spread_core]

    def slot(s):
        for stage in reversed(range(len(stages))):
            if 0 <= s - stage < 8:
                stages[stage](s - stage)

    tokens_x()
    basis_relay()
    send_shard_y(zl, grads_ref)
    z_step(1)
    own_a.wait()
    slot(0)
    tokens_core()
    z_step(2)
    relay_shard_y(zl)
    rotate_act()
    z_step(3)
    slot(1)
    relay_shard_y(mate)
    slot(2)
    slot(3)
    sum_act()
    relay_far()
    slot(4)
    act_y(1)
    slot(5)
    act_y(2)
    act_y(3)
    opposite_pair(near)
    slot(6)
    fit(0)
    for k in range(4):
        act_relay(k)
    opposite_pair(far)
    slot(7)
    fit(1)
    slot(8)
    fit(2)
    slot(9)
    fit(3)
    slot(10)
    fit(4)
    slot(11)
    fit(5)
    slot(12)
    act_opposite()
    fit(6)
    fit(7)
    copies.finish()


def call(arrays, x_type, r_type, collective_id):
    vmem = pl.BlockSpec(memory_space=pltpu.VMEM)
    dma = pltpu.SemaphoreType.DMA
    return pl.pallas_call(
        functools.partial(kernel, x_type, r_type),
        out_shape=jax.ShapeDtypeStruct((512, 896), F32),
        in_specs=[vmem] * 4,
        out_specs=vmem,
        scratch_shapes=[
            pltpu.VMEM((2048, 1792), BF16),
            pltpu.VMEM((8, 256, 896), F32),
            pltpu.VMEM((8, 128, 896), F32),
            pltpu.VMEM((8, 4, 32, 896), BF16),
            pltpu.VMEM((8, 3, 32, 896), x_type),
            pltpu.VMEM((8, 2, 16, 896), F32),
            pltpu.VMEM((8, 16, 896), F32),
            pltpu.VMEM((8, 256, 896), BF16),
            pltpu.VMEM((2048, 512), BF16),
            pltpu.VMEM((2, 4, 2, 128, 512), BF16),
            pltpu.VMEM((4, 128, 512), F32),
            pltpu.VMEM((4, 128, 512), BF16),
            pltpu.VMEM((3, 128, 512), r_type),
            pltpu.VMEM((16, 512, 128), BF16),
            dma((200,)),
            dma((3,)),
            dma((3, 4)),
            dma((2, 4)),
            dma((2,)),
            dma((2,)),
            dma((2, 2)),
            dma((4,)),
            dma((1,)),
            dma((3,)),
            dma((3,)),
            dma((2, 4)),
            dma((2, 4)),
            dma((8,)),
            dma((8, 3)),
            dma((8,)),
            dma((8,)),
            dma((8, 3)),
            dma((8,)),
        ],
        compiler_params=pltpu.CompilerParams(
            collective_id=collective_id, has_side_effects=True, vmem_limit_bytes=56 * 2**20
        ),
        cost_estimate=pl.CostEstimate(flops=9_600_000_000, bytes_accessed=6_000_000, transcendentals=0),
    )(*arrays)


def solution(mesh):
    in_specs = (P("dp", "tensor"), P("dp", "tensor"), P("dp", "tensor"), P("tensor", "dp"))
    out_specs = P("tensor", "dp")

    def local(*arrays):
        return call(arrays, F32, BF16, 0)

    return jax.shard_map(local, mesh=mesh, in_specs=in_specs, out_specs=out_specs, check_vma=False)
```

```python
import functools

import jax
import jax.numpy as jnp
from jax import lax
from jax.experimental import pallas as pl
from jax.experimental.pallas import tpu as pltpu
from jax.sharding import PartitionSpec as P

MESH = pl.DeviceIdType.MESH
F32 = jnp.float32
BF16 = jnp.bfloat16
SEQ = 128


class Copies:
    def __init__(self, send_sems):
        self.send_sems = send_sems
        self.sent = []

    def send(self, src, dst, recv_sem, to, cond=None, shared=None):
        index = len(self.sent)

        def build():
            return pltpu.make_async_remote_copy(
                src_ref=src,
                dst_ref=dst,
                send_sem=self.send_sems.at[index] if shared is None else shared,
                recv_sem=recv_sem,
                device_id=to,
                device_id_type=MESH,
            )

        if cond is None:
            build().start()
        else:
            pl.when(cond)(lambda: build().start())
        if shared is None:
            self.sent.append((build, cond))

    def finish(self):
        for build, cond in self.sent:
            if cond is None:
                build().wait_send()
            else:
                pl.when(cond)(lambda build=build: build().wait_send())


def kernel(
    r_type,
    tokens_ref, grads_ref, bin_ref, bout_ref, out_ref,
    a_all, part, core_in, x_in, x_sum, z_in, grad, b1, a1, r_part, r_out, r_in, rt,
    send_sems, local_sems, a_sem, a_half_sem, b1_sem, b1_half_sem, a1_first_sem, a1_x_sem, a1_core_sem,
    r_sem, r_send_sem, rt_z_sem, rt_y_sem, rt_y_send_sem, rt_half_sem, core_sem, x_sem, x_send_sem, z_sem, gx_sem, gx_send_sem, gc_sem,
):
    dp, tensor = lax.axis_index("dp"), lax.axis_index("tensor")
    y, zl = dp // 4, dp % 4
    zh, x, c = tensor // 8, (tensor // 2) % 4, tensor % 2

    def dev(x=x, y=y, zl=zl, zh=zh, c=c):
        return (y * 4 + zl, zh * 8 + x * 2 + c)

    def ring(v, k):
        return lax.rem(v + k + 4, 4)

    up_y, down_y = dev(y=ring(y, 1)), dev(y=ring(y, -1))
    core_mate, z_mate = dev(c=1 - c), dev(zh=1 - zh)
    x_others = [dev(x=ring(x, k)) for k in (1, 2, 3)]
    copies = Copies(send_sems)

    barrier = pltpu.get_barrier_semaphore()
    greeted = 0
    for dz in range(4):
        for dh in range(2):
            for dc in range(2):
                if dz or dh or dc:
                    pl.semaphore_signal(
                        barrier, inc=1, device_id=dev(zl=ring(zl, dz), zh=(zh + dh) % 2, c=(c + dc) % 2), device_id_type=MESH
                    )
                    greeted += 1
    for other in [up_y, down_y] + x_others:
        pl.semaphore_signal(barrier, inc=1, device_id=other, device_id_type=MESH)
        greeted += 1
    pl.semaphore_wait(barrier, greeted)

    def got(ref, sem):
        pltpu.make_async_copy(ref, ref, sem).wait()

    def shard(yy, zz):
        return a_all.at[pl.ds(pl.multiple_of((yy * 4 + zz) * SEQ, SEQ), SEQ)]

    def half_shard(yy, zz, half):
        return a_all.at[pl.ds(pl.multiple_of((yy * 4 + zz) * SEQ + half * (SEQ // 2), SEQ // 2), SEQ // 2)]

    def send_shard_y(zz, src, cond=None):
        copies.send(src, shard(y, zz), a_sem.at[1, zz], up_y, cond)
        copies.send(src, shard(y, zz), a_sem.at[2, zz], down_y, cond)

    low, high, opposite = ring(y, -1), ring(y, 1), ring(y, 2)

    def relay_shard_y(zz):
        got(shard(low, zz), a_sem.at[1, zz])
        copies.send(half_shard(low, zz, 0), half_shard(low, zz, 0), a_half_sem.at[0, zz], up_y)
        got(shard(high, zz), a_sem.at[2, zz])
        copies.send(half_shard(high, zz, 1), half_shard(high, zz, 1), a_half_sem.at[1, zz], down_y)

    z_target = 2 * (x % 2) + c
    a1_block = a1.at[zl % 2, 2 * zh + x // 2, zl // 2]
    for h in range(2):
        mine = jnp.logical_and(zl == z_target, zh == h)
        copies.send(
            tokens_ref, a1_block, a1_first_sem.at[zl // 2, zh], dev(zl=z_target, zh=h, c=zl % 2), jnp.logical_not(mine)
        )

        @pl.when(mine)
        def _():
            own = pltpu.make_async_copy(tokens_ref, a1_block, local_sems.at[2])
            own.start()
            own.wait()

    def b1_block(yy):
        return b1.at[pl.ds(pl.multiple_of(yy * 512, 512), 512)]

    def b1_half(yy, half):
        return b1.at[pl.ds(pl.multiple_of(yy * 512 + half * 256, 256), 256)]

    copies.send(bin_ref, b1_block(y), b1_sem.at[0], up_y)
    copies.send(bin_ref, b1_block(y), b1_sem.at[1], down_y)
    copies.send(grads_ref, shard(y, zl), a_sem.at[0, zl], dev(zl=jnp.minimum(zl + 1, 3)), zl < 3)
    copies.send(grads_ref, shard(y, zl), a_sem.at[0, zl], dev(zl=jnp.maximum(zl - 1, 0)), zl > 0)

    own_a = pltpu.make_async_copy(grads_ref, shard(y, zl), local_sems.at[0])
    own_b = pltpu.make_async_copy(bin_ref, b1_block(y), local_sems.at[1])
    own_a.start()
    own_b.start()

    def z_step(k):
        for sign in (-1, 1):
            source = zl + sign * k
            there = jnp.logical_and(source >= 0, source <= 3)
            zz = jnp.clip(source, 0, 3)
            pl.when(there)(lambda zz=zz: got(shard(y, zz), a_sem.at[0, zz]))
            if k < 3:
                onward = zl - sign
                copies.send(
                    shard(y, zz), shard(y, zz), a_sem.at[0, zz], dev(zl=jnp.clip(onward, 0, 3)),
                    jnp.logical_and(there, jnp.logical_and(onward >= 0, onward <= 3)),
                )
            send_shard_y(zz, shard(y, zz), there)

    parity = zl // 2

    def tokens_x():
        holds = x % 2 == parity
        for zhalf in range(2):
            for h in range(2):
                mine = jnp.logical_and(c + 2 * zhalf == zl, zh == h)
                pl.when(jnp.logical_and(holds, jnp.logical_not(mine)))(
                    lambda zhalf=zhalf, h=h: got(a1.at[c, 2 * h + x // 2, zhalf], a1_first_sem.at[zhalf, h])
                )
        for h in range(2):
            block = a1.at[c, 2 * h + x // 2]
            for other in x_others:
                copies.send(block, block, a1_x_sem.at[2 * h + x // 2], other, holds)

    def tokens_core():
        for kq in range(4):
            pl.when(parity + 2 * (kq % 2) != x)(lambda kq=kq: got(a1.at[c, kq], a1_x_sem.at[kq]))
        copies.send(a1.at[c], a1.at[c], a1_core_sem.at[0], core_mate)

    def basis_relay():
        got(b1_block(low), b1_sem.at[0])
        copies.send(b1_half(low, 0), b1_half(low, 0), b1_half_sem.at[0], up_y)
        got(b1_block(high), b1_sem.at[1])
        copies.send(b1_half(high, 1), b1_half(high, 1), b1_half_sem.at[1], down_y)

    near, far = zl // 2, 1 - zl // 2
    units = [(y, near), (y, far), (high, near), (low, near), (high, far), (low, far), (opposite, near), (opposite, far)]

    def rotate(i):
        g, h = units[i]
        rows = pl.ds(pl.multiple_of(g * 512 + h * 256, 256), 256)
        part[i] = jnp.dot(a_all[rows, :], bout_ref[...], preferred_element_type=F32)
        theirs = part.at[i, pl.ds(pl.multiple_of((1 - c) * 128, 128), 128)]
        copies.send(theirs, core_in.at[i], core_sem.at[i], core_mate)

    def sum_core(i):
        got(core_in.at[i], core_sem.at[i])
        rows = pl.ds(pl.multiple_of(c * 128, 128), 128)
        chip = part[i, rows, :] + core_in[i]
        part[i, rows, :] = chip
        for k, other in zip((1, 2, 3), x_others):
            piece = part.at[i, pl.ds(pl.multiple_of(c * 128 + ring(x, k) * 32, 32), 32)]
            copies.send(piece, x_in.at[i, k - 1], x_sem.at[i], other, shared=x_send_sem.at[i])

    def sum_x(i):
        got(x_in.at[i], x_sem.at[i])
        rows = pl.ds(pl.multiple_of(c * 128 + x * 32, 32), 32)
        x_sum[i] = (part[i, rows, :] + x_in[i, 0]) + (x_in[i, 1] + x_in[i, 2])
        copies.send(x_sum.at[i], z_in.at[i], z_sem.at[i], z_mate)

    def grad_rows(i, first, count):
        return grad.at[i, pl.ds(pl.multiple_of(first, count), count)]

    def sum_z(i):
        got(z_in.at[i], z_sem.at[i])
        first = c * 128 + x * 32
        grad[i, pl.ds(pl.multiple_of(first, 32), 32), :] = (x_sum[i] + z_in[i]).astype(BF16)
        own = grad_rows(i, first, 32)
        for other in x_others:
            copies.send(own, own, gx_sem.at[i], other, shared=gx_send_sem.at[i])

    def spread_core(i):
        got(grad.at[i, pl.ds(0, 96)], gx_sem.at[i])
        own = grad_rows(i, c * 128, 128)
        copies.send(own, own, gc_sem.at[i], core_mate)

    def fit(pair):
        examples = []
        for i in (2 * pair, 2 * pair + 1):
            got(grad_rows(i, (1 - c) * 128, 128), gc_sem.at[i])
            g, h = units[i]
            examples += [(g * 4 + h * 2 + n, i, n * SEQ) for n in range(2)]

        def tile(cols):
            total = None
            for example, i, first in examples:
                right = grad[i, first:first + SEQ, cols]
                product = jnp.dot(rt[example], right, preferred_element_type=F32)
                square = product * product
                total = square if total is None else total + square
            total = total * (1.0 / 2048)
            out_ref[:, cols] = total if pair == 0 else out_ref[:, cols] + total

        @pl.loop(0, 3)
        def _(j):
            tile(pl.ds(pl.multiple_of(j * 256, 256), 256))

        tile(pl.ds(768, 128))

    def place(zz):
        return (zz % 2) * 2 + zz // 2

    def rotate_act():
        own_b.wait()
        got(b1_half(opposite, 0), b1_half_sem.at[0])
        got(b1_half(opposite, 1), b1_half_sem.at[1])
        got(a1.at[1 - c], a1_core_sem.at[0])

        @pl.loop(0, 4)
        def _(kq):
            left = a1[:, kq].reshape(512, 512)
            right = b1[pl.ds(pl.multiple_of(kq * 512, 512), 512), :]
            term = jnp.dot(left, right, preferred_element_type=F32)

            @pl.when(kq == 0)
            def _():
                r_part[...] = term.reshape(4, SEQ, 512)

            @pl.when(kq != 0)
            def _():
                r_part[...] += term.reshape(4, SEQ, 512)

        source = r_part
        if r_type != F32:
            r_out[...] = r_part[...].astype(r_type)
            source = r_out
        for k in (1, 2, 3):
            zz = ring(zl, k)
            copies.send(source.at[place(zz)], r_in.at[k - 1], r_sem.at[0], dev(zl=zz), shared=r_send_sem.at[0])

    def r_block(yy, zz):
        return rt.at[yy * 4 + zz]

    def r_blocks(yy, first, count):
        return rt.at[pl.ds(yy * 4 + first, count)]

    def send_r_y(zz):
        copies.send(r_block(y, zz), r_block(y, zz), rt_y_sem.at[0], up_y, shared=rt_y_send_sem.at[0])
        copies.send(r_block(y, zz), r_block(y, zz), rt_y_sem.at[1], down_y, shared=rt_y_send_sem.at[1])

    def sum_act():
        got(r_in, r_sem.at[0])
        others = [r_in[k].astype(F32) for k in range(3)]
        own_r = (r_part[place(zl)] + others[0]) + (others[1] + others[2])
        rt[y * 4 + zl] = own_r.T.astype(BF16)
        for k in (1, 2, 3):
            copies.send(r_block(y, zl), r_block(y, zl), rt_z_sem.at[k - 1], dev(zl=ring(zl, k)))
        send_r_y(zl)

    def act_y(k):
        zz = ring(zl, -k)
        got(r_block(y, zz), rt_z_sem.at[k - 1])
        send_r_y(zz)

    def act_relay():
        got(r_blocks(low, 0, 4), rt_y_sem.at[0])
        copies.send(r_blocks(low, 0, 2), r_blocks(low, 0, 2), rt_half_sem.at[0], up_y)
        got(r_blocks(high, 0, 4), rt_y_sem.at[1])
        copies.send(r_blocks(high, 2, 2), r_blocks(high, 2, 2), rt_half_sem.at[1], down_y)

    def act_opposite():
        got(r_blocks(opposite, 0, 2), rt_half_sem.at[0])
        got(r_blocks(opposite, 2, 2), rt_half_sem.at[1])

    def finish_shared():
        for i in range(8):
            got(x_in.at[i], x_send_sem.at[i])
            got(grad.at[i, pl.ds(0, 96)], gx_send_sem.at[i])
        got(r_in, r_send_sem.at[0])
        for side in range(2):
            got(r_blocks(y, 0, 4), rt_y_send_sem.at[side])

    def opposite_pair(h):
        for k in range(2):
            got(half_shard(opposite, 2 * h + k, 0), a_half_sem.at[0, 2 * h + k])
            got(half_shard(opposite, 2 * h + k, 1), a_half_sem.at[1, 2 * h + k])

    mate = zl + 1 - 2 * (zl % 2)

    def relay_far():
        relay_shard_y(2 * far)
        relay_shard_y(2 * far + 1)

    stages = [rotate, sum_core, sum_x, sum_z, spread_core]

    def slot(s):
        for stage in reversed(range(len(stages))):
            if 0 <= s - stage < 8:
                stages[stage](s - stage)

    tokens_x()
    basis_relay()
    send_shard_y(zl, grads_ref)
    z_step(1)
    own_a.wait()
    slot(0)
    z_step(2)
    tokens_core()
    relay_shard_y(zl)
    rotate_act()
    z_step(3)
    slot(1)
    relay_shard_y(mate)
    slot(2)
    slot(3)
    sum_act()
    relay_far()
    slot(4)
    act_y(1)
    slot(5)
    act_y(2)
    act_y(3)
    opposite_pair(near)
    slot(6)
    act_relay()
    opposite_pair(far)
    slot(7)
    fit(0)
    slot(8)
    fit(1)
    slot(9)
    fit(2)
    slot(10)
    slot(11)
    act_opposite()
    fit(3)
    finish_shared()
    copies.finish()


def call(arrays, r_type, collective_id):
    vmem = pl.BlockSpec(memory_space=pltpu.VMEM)
    dma = pltpu.SemaphoreType.DMA
    return pl.pallas_call(
        functools.partial(kernel, r_type),
        out_shape=jax.ShapeDtypeStruct((512, 896), F32),
        in_specs=[vmem] * 4,
        out_specs=vmem,
        scratch_shapes=[
            pltpu.VMEM((2048, 1792), BF16),
            pltpu.VMEM((8, 256, 896), F32),
            pltpu.VMEM((8, 128, 896), F32),
            pltpu.VMEM((8, 3, 32, 896), F32),
            pltpu.VMEM((8, 32, 896), F32),
            pltpu.VMEM((8, 32, 896), F32),
            pltpu.VMEM((8, 256, 896), BF16),
            pltpu.VMEM((2048, 512), BF16),
            pltpu.VMEM((2, 4, 2, 128, 512), BF16),
            pltpu.VMEM((4, 128, 512), F32),
            pltpu.VMEM((4, 128, 512), BF16),
            pltpu.VMEM((3, 128, 512), r_type),
            pltpu.VMEM((16, 512, 128), BF16),
            dma((200,)),
            dma((3,)),
            dma((3, 4)),
            dma((2, 4)),
            dma((2,)),
            dma((2,)),
            dma((2, 2)),
            dma((4,)),
            dma((1,)),
            dma((1,)),
            dma((1,)),
            dma((3,)),
            dma((2,)),
            dma((2,)),
            dma((2,)),
            dma((8,)),
            dma((8,)),
            dma((8,)),
            dma((8,)),
            dma((8,)),
            dma((8,)),
            dma((8,)),
        ],
        compiler_params=pltpu.CompilerParams(
            collective_id=collective_id, has_side_effects=True, vmem_limit_bytes=56 * 2**20
        ),
        cost_estimate=pl.CostEstimate(flops=9_600_000_000, bytes_accessed=6_000_000, transcendentals=0),
    )(*arrays)


def solution(mesh):
    in_specs = (P("dp", "tensor"), P("dp", "tensor"), P("dp", "tensor"), P("tensor", "dp"))
    out_specs = P("tensor", "dp")

    def local(*arrays):
        return call(arrays, BF16, 0)

    return jax.shard_map(local, mesh=mesh, in_specs=in_specs, out_specs=out_specs, check_vma=False)
```

```python
import functools

import jax
import jax.numpy as jnp
from jax import lax
from jax.experimental import pallas as pl
from jax.experimental.pallas import tpu as pltpu
from jax.sharding import PartitionSpec as P

MESH = pl.DeviceIdType.MESH
F32 = jnp.float32
BF16 = jnp.bfloat16
SEQ = 128


class Copies:
    def __init__(self, send_sems):
        self.send_sems = send_sems
        self.sent = []

    def send(self, src, dst, recv_sem, to, cond=None, shared=None):
        index = len(self.sent)

        def build():
            return pltpu.make_async_remote_copy(
                src_ref=src,
                dst_ref=dst,
                send_sem=self.send_sems.at[index] if shared is None else shared,
                recv_sem=recv_sem,
                device_id=to,
                device_id_type=MESH,
            )

        if cond is None:
            build().start()
        else:
            pl.when(cond)(lambda: build().start())
        if shared is None:
            self.sent.append((build, cond))

    def finish(self):
        for build, cond in self.sent:
            if cond is None:
                build().wait_send()
            else:
                pl.when(cond)(lambda build=build: build().wait_send())


def kernel(
    r_type,
    tokens_ref, grads_ref, bin_ref, bout_ref, out_ref,
    a_all, part, core_in, x_in, x_sum, z_in, grad, b1, a1, r_part, r_out, r_in, rt,
    send_sems, local_sems, a_sem, a_half_sem, b1_sem, b1_half_sem, a1_first_sem, a1_x_sem, a1_core_sem,
    r_sem, r_send_sem, rt_z_sem, rt_y_sem, rt_y_send_sem, rt_half_sem, core_sem, x_sem, x_send_sem, z_sem, gx_sem, gx_send_sem, gc_sem,
):
    dp, tensor = lax.axis_index("dp"), lax.axis_index("tensor")
    y, zl = dp // 4, dp % 4
    zh, x, c = tensor // 8, (tensor // 2) % 4, tensor % 2

    def dev(x=x, y=y, zl=zl, zh=zh, c=c):
        return (y * 4 + zl, zh * 8 + x * 2 + c)

    def ring(v, k):
        return lax.rem(v + k + 4, 4)

    up_y, down_y = dev(y=ring(y, 1)), dev(y=ring(y, -1))
    core_mate, z_mate = dev(c=1 - c), dev(zh=1 - zh)
    x_others = [dev(x=ring(x, k)) for k in (1, 2, 3)]
    copies = Copies(send_sems)

    barrier = pltpu.get_barrier_semaphore()
    greeted = 0
    for dz in range(4):
        for dh in range(2):
            for dc in range(2):
                if dz or dh or dc:
                    pl.semaphore_signal(
                        barrier, inc=1, device_id=dev(zl=ring(zl, dz), zh=(zh + dh) % 2, c=(c + dc) % 2), device_id_type=MESH
                    )
                    greeted += 1
    for other in [up_y, down_y] + x_others:
        pl.semaphore_signal(barrier, inc=1, device_id=other, device_id_type=MESH)
        greeted += 1
    pl.semaphore_wait(barrier, greeted)

    def got(ref, sem):
        pltpu.make_async_copy(ref, ref, sem).wait()

    def shard(yy, zz):
        return a_all.at[pl.ds(pl.multiple_of((yy * 4 + zz) * SEQ, SEQ), SEQ)]

    def half_shard(yy, zz, half):
        return a_all.at[pl.ds(pl.multiple_of((yy * 4 + zz) * SEQ + half * (SEQ // 2), SEQ // 2), SEQ // 2)]

    def send_shard_y(zz, src, cond=None):
        copies.send(src, shard(y, zz), a_sem.at[1, zz], up_y, cond)
        copies.send(src, shard(y, zz), a_sem.at[2, zz], down_y, cond)

    low, high, opposite = ring(y, -1), ring(y, 1), ring(y, 2)

    def relay_shard_y(zz):
        got(shard(low, zz), a_sem.at[1, zz])
        copies.send(half_shard(low, zz, 0), half_shard(low, zz, 0), a_half_sem.at[0, zz], up_y)
        got(shard(high, zz), a_sem.at[2, zz])
        copies.send(half_shard(high, zz, 1), half_shard(high, zz, 1), a_half_sem.at[1, zz], down_y)

    z_target = 2 * (x % 2) + c
    a1_block = a1.at[zl % 2, 2 * zh + x // 2, zl // 2]
    for h in range(2):
        mine = jnp.logical_and(zl == z_target, zh == h)
        copies.send(
            tokens_ref, a1_block, a1_first_sem.at[zl // 2, zh], dev(zl=z_target, zh=h, c=zl % 2), jnp.logical_not(mine)
        )

        @pl.when(mine)
        def _():
            own = pltpu.make_async_copy(tokens_ref, a1_block, local_sems.at[2])
            own.start()
            own.wait()

    def b1_block(yy):
        return b1.at[pl.ds(pl.multiple_of(yy * 512, 512), 512)]

    def b1_half(yy, half):
        return b1.at[pl.ds(pl.multiple_of(yy * 512 + half * 256, 256), 256)]

    copies.send(bin_ref, b1_block(y), b1_sem.at[0], up_y)
    copies.send(bin_ref, b1_block(y), b1_sem.at[1], down_y)
    copies.send(grads_ref, shard(y, zl), a_sem.at[0, zl], dev(zl=jnp.minimum(zl + 1, 3)), zl < 3)
    copies.send(grads_ref, shard(y, zl), a_sem.at[0, zl], dev(zl=jnp.maximum(zl - 1, 0)), zl > 0)

    own_a = pltpu.make_async_copy(grads_ref, shard(y, zl), local_sems.at[0])
    own_b = pltpu.make_async_copy(bin_ref, b1_block(y), local_sems.at[1])
    own_a.start()
    own_b.start()

    def z_step(k):
        for sign in (-1, 1):
            source = zl + sign * k
            there = jnp.logical_and(source >= 0, source <= 3)
            zz = jnp.clip(source, 0, 3)
            pl.when(there)(lambda zz=zz: got(shard(y, zz), a_sem.at[0, zz]))
            if k < 3:
                onward = zl - sign
                copies.send(
                    shard(y, zz), shard(y, zz), a_sem.at[0, zz], dev(zl=jnp.clip(onward, 0, 3)),
                    jnp.logical_and(there, jnp.logical_and(onward >= 0, onward <= 3)),
                )
            send_shard_y(zz, shard(y, zz), there)

    parity = zl // 2

    def tokens_x():
        holds = x % 2 == parity
        for zhalf in range(2):
            for h in range(2):
                mine = jnp.logical_and(c + 2 * zhalf == zl, zh == h)
                pl.when(jnp.logical_and(holds, jnp.logical_not(mine)))(
                    lambda zhalf=zhalf, h=h: got(a1.at[c, 2 * h + x // 2, zhalf], a1_first_sem.at[zhalf, h])
                )
        for h in range(2):
            block = a1.at[c, 2 * h + x // 2]
            for other in x_others:
                copies.send(block, block, a1_x_sem.at[2 * h + x // 2], other, holds)

    def tokens_core():
        for kq in range(4):
            pl.when(parity + 2 * (kq % 2) != x)(lambda kq=kq: got(a1.at[c, kq], a1_x_sem.at[kq]))
        copies.send(a1.at[c], a1.at[c], a1_core_sem.at[0], core_mate)

    def basis_relay():
        got(b1_block(low), b1_sem.at[0])
        copies.send(b1_half(low, 0), b1_half(low, 0), b1_half_sem.at[0], up_y)
        got(b1_block(high), b1_sem.at[1])
        copies.send(b1_half(high, 1), b1_half(high, 1), b1_half_sem.at[1], down_y)

    near, far = zl // 2, 1 - zl // 2
    units = [(y, near), (y, far), (high, near), (low, near), (high, far), (low, far), (opposite, near), (opposite, far)]

    def rotate(i):
        g, h = units[i]
        rows = pl.ds(pl.multiple_of(g * 512 + h * 256, 256), 256)
        part[i] = jnp.dot(a_all[rows, :], bout_ref[...], preferred_element_type=F32)
        theirs = part.at[i, pl.ds(pl.multiple_of((1 - c) * 128, 128), 128)]
        copies.send(theirs, core_in.at[i], core_sem.at[i], core_mate)

    def sum_core(i):
        got(core_in.at[i], core_sem.at[i])
        rows = pl.ds(pl.multiple_of(c * 128, 128), 128)
        chip = part[i, rows, :] + core_in[i]
        part[i, rows, :] = chip
        for k, other in zip((1, 2, 3), x_others):
            piece = part.at[i, pl.ds(pl.multiple_of(c * 128 + ring(x, k) * 32, 32), 32)]
            copies.send(piece, x_in.at[i, k - 1], x_sem.at[i], other, shared=x_send_sem.at[i])

    def sum_x(i):
        got(x_in.at[i], x_sem.at[i])
        rows = pl.ds(pl.multiple_of(c * 128 + x * 32, 32), 32)
        x_sum[i] = (part[i, rows, :] + x_in[i, 0]) + (x_in[i, 1] + x_in[i, 2])
        copies.send(x_sum.at[i], z_in.at[i], z_sem.at[i], z_mate)

    def grad_rows(i, first, count):
        return grad.at[i, pl.ds(pl.multiple_of(first, count), count)]

    def sum_z(i):
        got(z_in.at[i], z_sem.at[i])
        first = c * 128 + x * 32
        grad[i, pl.ds(pl.multiple_of(first, 32), 32), :] = (x_sum[i] + z_in[i]).astype(BF16)
        own = grad_rows(i, first, 32)
        for other in x_others:
            copies.send(own, own, gx_sem.at[i], other, shared=gx_send_sem.at[i])

    def spread_core(i):
        got(grad.at[i, pl.ds(0, 96)], gx_sem.at[i])
        own = grad_rows(i, c * 128, 128)
        copies.send(own, own, gc_sem.at[i], core_mate)

    def fit(pair):
        examples = []
        for i in (2 * pair, 2 * pair + 1):
            got(grad_rows(i, (1 - c) * 128, 128), gc_sem.at[i])
            g, h = units[i]
            examples += [(g * 4 + h * 2 + n, i, n * SEQ) for n in range(2)]

        def tile(cols):
            total = None
            for example, i, first in examples:
                right = grad[i, first:first + SEQ, cols]
                product = jnp.dot(rt[example], right, preferred_element_type=F32)
                square = product * product
                total = square if total is None else total + square
            total = total * (1.0 / 2048)
            out_ref[:, cols] = total if pair == 0 else out_ref[:, cols] + total

        @pl.loop(0, 3)
        def _(j):
            tile(pl.ds(pl.multiple_of(j * 256, 256), 256))

        tile(pl.ds(768, 128))

    def place(zz):
        return (zz % 2) * 2 + zz // 2

    def rotate_act():
        own_b.wait()
        got(b1_half(opposite, 0), b1_half_sem.at[0])
        got(b1_half(opposite, 1), b1_half_sem.at[1])
        got(a1.at[1 - c], a1_core_sem.at[0])

        @pl.loop(0, 4)
        def _(kq):
            left = a1[:, kq].reshape(512, 512)
            right = b1[pl.ds(pl.multiple_of(kq * 512, 512), 512), :]
            term = jnp.dot(left, right, preferred_element_type=F32)

            @pl.when(kq == 0)
            def _():
                r_part[...] = term.reshape(4, SEQ, 512)

            @pl.when(kq != 0)
            def _():
                r_part[...] += term.reshape(4, SEQ, 512)

        source = r_part
        if r_type != F32:
            r_out[...] = r_part[...].astype(r_type)
            source = r_out
        for k in (1, 2, 3):
            zz = ring(zl, k)
            copies.send(source.at[place(zz)], r_in.at[k - 1], r_sem.at[0], dev(zl=zz), shared=r_send_sem.at[0])

    def r_block(yy, zz):
        return rt.at[yy * 4 + zz]

    def r_blocks(yy, first, count):
        return rt.at[pl.ds(yy * 4 + first, count)]

    def send_r_y(zz):
        copies.send(r_block(y, zz), r_block(y, zz), rt_y_sem.at[0], up_y, shared=rt_y_send_sem.at[0])
        copies.send(r_block(y, zz), r_block(y, zz), rt_y_sem.at[1], down_y, shared=rt_y_send_sem.at[1])

    def sum_act():
        got(r_in, r_sem.at[0])
        others = [r_in[k].astype(F32) for k in range(3)]
        own_r = (r_part[place(zl)] + others[0]) + (others[1] + others[2])
        rt[y * 4 + zl] = own_r.T.astype(BF16)
        for k in (1, 2, 3):
            copies.send(r_block(y, zl), r_block(y, zl), rt_z_sem.at[k - 1], dev(zl=ring(zl, k)))
        send_r_y(zl)

    def act_y(k):
        zz = ring(zl, -k)
        got(r_block(y, zz), rt_z_sem.at[k - 1])
        send_r_y(zz)

    def act_relay():
        got(r_blocks(low, 0, 4), rt_y_sem.at[0])
        copies.send(r_blocks(low, 0, 2), r_blocks(low, 0, 2), rt_half_sem.at[0], up_y)
        got(r_blocks(high, 0, 4), rt_y_sem.at[1])
        copies.send(r_blocks(high, 2, 2), r_blocks(high, 2, 2), rt_half_sem.at[1], down_y)

    def act_opposite():
        got(r_blocks(opposite, 0, 2), rt_half_sem.at[0])
        got(r_blocks(opposite, 2, 2), rt_half_sem.at[1])

    def finish_shared():
        for i in range(8):
            got(x_in.at[i], x_send_sem.at[i])
            got(grad.at[i, pl.ds(0, 96)], gx_send_sem.at[i])
        got(r_in, r_send_sem.at[0])
        for side in range(2):
            got(r_blocks(y, 0, 4), rt_y_send_sem.at[side])

    def opposite_pair(h):
        for k in range(2):
            got(half_shard(opposite, 2 * h + k, 0), a_half_sem.at[0, 2 * h + k])
            got(half_shard(opposite, 2 * h + k, 1), a_half_sem.at[1, 2 * h + k])

    mate = zl + 1 - 2 * (zl % 2)

    def relay_far():
        relay_shard_y(2 * far)
        relay_shard_y(2 * far + 1)

    stages = [rotate, sum_core, sum_x, sum_z, spread_core]

    def slot(s):
        for stage in reversed(range(len(stages))):
            if 0 <= s - stage < 8:
                stages[stage](s - stage)

    tokens_x()
    basis_relay()
    send_shard_y(zl, grads_ref)
    z_step(1)
    own_a.wait()
    rotate(0)
    sum_core(0)
    z_step(2)
    tokens_core()
    relay_shard_y(zl)
    rotate_act()
    z_step(3)
    sum_x(0)
    rotate(1)
    relay_shard_y(mate)
    sum_core(1)
    rotate(2)
    rotate(3)
    sum_z(0)
    sum_core(2)
    sum_core(3)
    sum_x(1)
    sum_act()
    relay_far()
    spread_core(0)
    sum_z(1)
    sum_x(2)
    sum_x(3)
    rotate(4)
    rotate(5)
    sum_core(4)
    sum_core(5)
    act_y(1)
    act_y(2)
    act_y(3)
    spread_core(1)
    sum_z(2)
    sum_z(3)
    sum_x(4)
    sum_x(5)
    opposite_pair(near)
    rotate(6)
    sum_core(6)
    spread_core(2)
    spread_core(3)
    sum_z(4)
    sum_z(5)
    opposite_pair(far)
    rotate(7)
    sum_core(7)
    act_relay()
    sum_x(6)
    fit(0)
    spread_core(4)
    spread_core(5)
    sum_x(7)
    sum_z(6)
    fit(1)
    sum_z(7)
    spread_core(6)
    fit(2)
    spread_core(7)
    act_opposite()
    fit(3)
    finish_shared()
    copies.finish()


def call(arrays, r_type, collective_id):
    vmem = pl.BlockSpec(memory_space=pltpu.VMEM)
    dma = pltpu.SemaphoreType.DMA
    return pl.pallas_call(
        functools.partial(kernel, r_type),
        out_shape=jax.ShapeDtypeStruct((512, 896), F32),
        in_specs=[vmem] * 4,
        out_specs=vmem,
        scratch_shapes=[
            pltpu.VMEM((2048, 1792), BF16),
            pltpu.VMEM((8, 256, 896), F32),
            pltpu.VMEM((8, 128, 896), F32),
            pltpu.VMEM((8, 3, 32, 896), F32),
            pltpu.VMEM((8, 32, 896), F32),
            pltpu.VMEM((8, 32, 896), F32),
            pltpu.VMEM((8, 256, 896), BF16),
            pltpu.VMEM((2048, 512), BF16),
            pltpu.VMEM((2, 4, 2, 128, 512), BF16),
            pltpu.VMEM((4, 128, 512), F32),
            pltpu.VMEM((4, 128, 512), BF16),
            pltpu.VMEM((3, 128, 512), r_type),
            pltpu.VMEM((16, 512, 128), BF16),
            dma((200,)),
            dma((3,)),
            dma((3, 4)),
            dma((2, 4)),
            dma((2,)),
            dma((2,)),
            dma((2, 2)),
            dma((4,)),
            dma((1,)),
            dma((1,)),
            dma((1,)),
            dma((3,)),
            dma((2,)),
            dma((2,)),
            dma((2,)),
            dma((8,)),
            dma((8,)),
            dma((8,)),
            dma((8,)),
            dma((8,)),
            dma((8,)),
            dma((8,)),
        ],
        compiler_params=pltpu.CompilerParams(
            collective_id=collective_id, has_side_effects=True, vmem_limit_bytes=56 * 2**20
        ),
        cost_estimate=pl.CostEstimate(flops=9_600_000_000, bytes_accessed=6_000_000, transcendentals=0),
    )(*arrays)


def solution(mesh):
    in_specs = (P("dp", "tensor"), P("dp", "tensor"), P("dp", "tensor"), P("tensor", "dp"))
    out_specs = P("tensor", "dp")

    def local(*arrays):
        return call(arrays, BF16, 0)

    return jax.shard_map(local, mesh=mesh, in_specs=in_specs, out_specs=out_specs, check_vma=False)
```

```python
import functools

import jax
import jax.numpy as jnp
from jax import lax
from jax.experimental import pallas as pl
from jax.experimental.pallas import tpu as pltpu
from jax.sharding import PartitionSpec as P

MESH = pl.DeviceIdType.MESH
F32 = jnp.float32
BF16 = jnp.bfloat16
SEQ = 128


class Copies:
    def __init__(self, send_sems):
        self.send_sems = send_sems
        self.sent = []
        self.count = 0

    def send(self, src, dst, recv_sem, to, cond=None, shared=None):
        index = self.count

        def build():
            return pltpu.make_async_remote_copy(
                src_ref=src,
                dst_ref=dst,
                send_sem=self.send_sems.at[index] if shared is None else shared,
                recv_sem=recv_sem,
                device_id=to,
                device_id_type=MESH,
            )

        if cond is None:
            build().start()
        else:
            pl.when(cond)(lambda: build().start())
        if shared is None:
            self.count += 1
            self.sent.append((build, cond))

    def finish(self, keep=0):
        done = self.sent[:len(self.sent) - keep]
        self.sent = self.sent[len(done):]
        for build, cond in done:
            if cond is None:
                build().wait_send()
            else:
                pl.when(cond)(lambda build=build: build().wait_send())


def kernel(
    r_type,
    tokens_ref, grads_ref, bin_ref, bout_hbm, out_ref,
    a_all, part, core_in, x_in, x_sum, z_in, grad, b1, a1, r_part, r_out, r_in, rt,
    bout_ref, send_sems, local_sems, a_sem, a_half_sem, b1_sem, b1_half_sem, a1_first_sem, a1_x_sem, a1_core_sem,
    r_sem, r_send_sem, rt_z_sem, rt_y_sem, rt_y_send_sem, rt_half_sem, core_sem, x_sem, x_send_sem, z_sem, gx_sem, gx_send_sem, gc_sem,
):
    dp, tensor = lax.axis_index("dp"), lax.axis_index("tensor")
    y, zl = dp // 4, dp % 4
    zh, x, c = tensor // 8, (tensor // 2) % 4, tensor % 2

    def dev(x=x, y=y, zl=zl, zh=zh, c=c):
        return (y * 4 + zl, zh * 8 + x * 2 + c)

    def ring(v, k):
        return lax.rem(v + k + 4, 4)

    up_y, down_y = dev(y=ring(y, 1)), dev(y=ring(y, -1))
    core_mate, z_mate = dev(c=1 - c), dev(zh=1 - zh)
    x_others = [dev(x=ring(x, k)) for k in (1, 2, 3)]
    copies = Copies(send_sems)

    own_basis = pltpu.make_async_copy(bout_hbm, bout_ref, local_sems.at[3])
    own_basis.start()

    barrier = pltpu.get_barrier_semaphore()
    greeted = 0
    for dz in range(4):
        for dh in range(2):
            for dc in range(2):
                if dz or dh or dc:
                    pl.semaphore_signal(
                        barrier, inc=1, device_id=dev(zl=ring(zl, dz), zh=(zh + dh) % 2, c=(c + dc) % 2), device_id_type=MESH
                    )
                    greeted += 1
    for other in [up_y, down_y] + x_others:
        pl.semaphore_signal(barrier, inc=1, device_id=other, device_id_type=MESH)
        greeted += 1
    pl.semaphore_wait(barrier, greeted)

    def got(ref, sem):
        pltpu.make_async_copy(ref, ref, sem).wait()

    def shard(yy, zz):
        return a_all.at[pl.ds(pl.multiple_of((yy * 4 + zz) * SEQ, SEQ), SEQ)]

    def half_shard(yy, zz, half):
        return a_all.at[pl.ds(pl.multiple_of((yy * 4 + zz) * SEQ + half * (SEQ // 2), SEQ // 2), SEQ // 2)]

    def send_shard_y(zz, src, cond=None):
        copies.send(src, shard(y, zz), a_sem.at[1, zz], up_y, cond)
        copies.send(src, shard(y, zz), a_sem.at[2, zz], down_y, cond)

    low, high, opposite = ring(y, -1), ring(y, 1), ring(y, 2)

    def relay_shard_y(zz):
        got(shard(low, zz), a_sem.at[1, zz])
        copies.send(half_shard(low, zz, 0), half_shard(low, zz, 0), a_half_sem.at[0, zz], up_y)
        got(shard(high, zz), a_sem.at[2, zz])
        copies.send(half_shard(high, zz, 1), half_shard(high, zz, 1), a_half_sem.at[1, zz], down_y)

    z_target = 2 * (x % 2) + c
    a1_block = a1.at[zl % 2, 2 * zh + x // 2, zl // 2]
    for h in range(2):
        mine = jnp.logical_and(zl == z_target, zh == h)
        copies.send(
            tokens_ref, a1_block, a1_first_sem.at[zl // 2, zh], dev(zl=z_target, zh=h, c=zl % 2), jnp.logical_not(mine)
        )

        @pl.when(mine)
        def _():
            own = pltpu.make_async_copy(tokens_ref, a1_block, local_sems.at[2])
            own.start()
            own.wait()

    def b1_block(yy):
        return b1.at[pl.ds(pl.multiple_of(yy * 512, 512), 512)]

    def b1_half(yy, half):
        return b1.at[pl.ds(pl.multiple_of(yy * 512 + half * 256, 256), 256)]

    copies.send(bin_ref, b1_block(y), b1_sem.at[0], up_y)
    copies.send(bin_ref, b1_block(y), b1_sem.at[1], down_y)
    copies.send(grads_ref, shard(y, zl), a_sem.at[0, zl], dev(zl=jnp.minimum(zl + 1, 3)), zl < 3)
    copies.send(grads_ref, shard(y, zl), a_sem.at[0, zl], dev(zl=jnp.maximum(zl - 1, 0)), zl > 0)

    own_a = pltpu.make_async_copy(grads_ref, shard(y, zl), local_sems.at[0])
    own_b = pltpu.make_async_copy(bin_ref, b1_block(y), local_sems.at[1])
    own_a.start()
    own_b.start()

    def z_step(k):
        for sign in (-1, 1):
            source = zl + sign * k
            there = jnp.logical_and(source >= 0, source <= 3)
            zz = jnp.clip(source, 0, 3)
            pl.when(there)(lambda zz=zz: got(shard(y, zz), a_sem.at[0, zz]))
            if k < 3:
                onward = zl - sign
                copies.send(
                    shard(y, zz), shard(y, zz), a_sem.at[0, zz], dev(zl=jnp.clip(onward, 0, 3)),
                    jnp.logical_and(there, jnp.logical_and(onward >= 0, onward <= 3)),
                )
            send_shard_y(zz, shard(y, zz), there)

    parity = zl // 2

    def tokens_x():
        holds = x % 2 == parity
        for zhalf in range(2):
            for h in range(2):
                mine = jnp.logical_and(c + 2 * zhalf == zl, zh == h)
                pl.when(jnp.logical_and(holds, jnp.logical_not(mine)))(
                    lambda zhalf=zhalf, h=h: got(a1.at[c, 2 * h + x // 2, zhalf], a1_first_sem.at[zhalf, h])
                )
        for h in range(2):
            block = a1.at[c, 2 * h + x // 2]
            for other in x_others:
                copies.send(block, block, a1_x_sem.at[2 * h + x // 2], other, holds)

    def tokens_core():
        for kq in range(4):
            pl.when(parity + 2 * (kq % 2) != x)(lambda kq=kq: got(a1.at[c, kq], a1_x_sem.at[kq]))
        copies.send(a1.at[c], a1.at[c], a1_core_sem.at[0], core_mate)

    def basis_relay():
        got(b1_block(low), b1_sem.at[0])
        copies.send(b1_half(low, 0), b1_half(low, 0), b1_half_sem.at[0], up_y)
        got(b1_block(high), b1_sem.at[1])
        copies.send(b1_half(high, 1), b1_half(high, 1), b1_half_sem.at[1], down_y)

    near, far = zl // 2, 1 - zl // 2
    units = [(y, near), (y, far), (high, near), (low, near), (high, far), (low, far), (opposite, near), (opposite, far)]

    def rotate(i):
        g, h = units[i]
        rows = pl.ds(pl.multiple_of(g * 512 + h * 256, 256), 256)
        part[i] = jnp.dot(a_all[rows, :], bout_ref[...], preferred_element_type=F32)
        theirs = part.at[i, pl.ds(pl.multiple_of((1 - c) * 128, 128), 128)]
        copies.send(theirs, core_in.at[i], core_sem.at[i], core_mate)

    def sum_core(i):
        got(core_in.at[i], core_sem.at[i])
        rows = pl.ds(pl.multiple_of(c * 128, 128), 128)
        chip = part[i, rows, :] + core_in[i]
        part[i, rows, :] = chip
        for k, other in zip((1, 2, 3), x_others):
            piece = part.at[i, pl.ds(pl.multiple_of(c * 128 + ring(x, k) * 32, 32), 32)]
            copies.send(piece, x_in.at[i, k - 1], x_sem.at[i], other, shared=x_send_sem.at[i])

    def sum_x(i):
        got(x_in.at[i], x_sem.at[i])
        rows = pl.ds(pl.multiple_of(c * 128 + x * 32, 32), 32)
        x_sum[i] = (part[i, rows, :] + x_in[i, 0]) + (x_in[i, 1] + x_in[i, 2])
        copies.send(x_sum.at[i], z_in.at[i], z_sem.at[i], z_mate)

    def grad_rows(i, first, count):
        return grad.at[i, pl.ds(pl.multiple_of(first, count), count)]

    def sum_z(i):
        got(z_in.at[i], z_sem.at[i])
        first = c * 128 + x * 32
        grad[i, pl.ds(pl.multiple_of(first, 32), 32), :] = (x_sum[i] + z_in[i]).astype(BF16)
        own = grad_rows(i, first, 32)
        for other in x_others:
            copies.send(own, own, gx_sem.at[i], other, shared=gx_send_sem.at[i])

    def spread_core(i):
        got(grad.at[i, pl.ds(0, 96)], gx_sem.at[i])
        own = grad_rows(i, c * 128, 128)
        copies.send(own, own, gc_sem.at[i], core_mate)

    def fit(pair):
        examples = []
        for i in (2 * pair, 2 * pair + 1):
            got(grad_rows(i, (1 - c) * 128, 128), gc_sem.at[i])
            g, h = units[i]
            examples += [(g * 4 + h * 2 + n, i, n * SEQ) for n in range(2)]

        def tile(cols):
            total = None
            for example, i, first in examples:
                right = grad[i, first:first + SEQ, cols]
                product = jnp.dot(rt[example], right, preferred_element_type=F32)
                square = product * product
                total = square if total is None else total + square
            total = total * (1.0 / 2048)
            out_ref[:, cols] = total if pair == 0 else out_ref[:, cols] + total

        @pl.loop(0, 3)
        def _(j):
            tile(pl.ds(pl.multiple_of(j * 256, 256), 256))

        tile(pl.ds(768, 128))

    def place(zz):
        return (zz % 2) * 2 + zz // 2

    def rotate_act():
        own_b.wait()
        got(b1_half(opposite, 0), b1_half_sem.at[0])
        got(b1_half(opposite, 1), b1_half_sem.at[1])
        got(a1.at[1 - c], a1_core_sem.at[0])

        @pl.loop(0, 4)
        def _(kq):
            left = a1[:, kq].reshape(512, 512)
            right = b1[pl.ds(pl.multiple_of(kq * 512, 512), 512), :]
            term = jnp.dot(left, right, preferred_element_type=F32)

            @pl.when(kq == 0)
            def _():
                r_part[...] = term.reshape(4, SEQ, 512)

            @pl.when(kq != 0)
            def _():
                r_part[...] += term.reshape(4, SEQ, 512)

        source = r_part
        if r_type != F32:
            r_out[...] = r_part[...].astype(r_type)
            source = r_out
        for k in (1, 2, 3):
            zz = ring(zl, k)
            copies.send(source.at[place(zz)], r_in.at[k - 1], r_sem.at[0], dev(zl=zz), shared=r_send_sem.at[0])

    def r_block(yy, zz):
        return rt.at[yy * 4 + zz]

    def r_blocks(yy, first, count):
        return rt.at[pl.ds(yy * 4 + first, count)]

    def send_r_y(zz):
        copies.send(r_block(y, zz), r_block(y, zz), rt_y_sem.at[0], up_y, shared=rt_y_send_sem.at[0])
        copies.send(r_block(y, zz), r_block(y, zz), rt_y_sem.at[1], down_y, shared=rt_y_send_sem.at[1])

    def sum_act():
        got(r_in, r_sem.at[0])
        others = [r_in[k].astype(F32) for k in range(3)]
        own_r = (r_part[place(zl)] + others[0]) + (others[1] + others[2])
        rt[y * 4 + zl] = own_r.T.astype(BF16)
        for k in (1, 2, 3):
            copies.send(r_block(y, zl), r_block(y, zl), rt_z_sem.at[k - 1], dev(zl=ring(zl, k)))
        send_r_y(zl)

    def act_y(k):
        zz = ring(zl, -k)
        got(r_block(y, zz), rt_z_sem.at[k - 1])
        send_r_y(zz)

    def act_relay():
        got(r_blocks(low, 0, 4), rt_y_sem.at[0])
        copies.send(r_blocks(low, 0, 2), r_blocks(low, 0, 2), rt_half_sem.at[0], up_y)
        got(r_blocks(high, 0, 4), rt_y_sem.at[1])
        copies.send(r_blocks(high, 2, 2), r_blocks(high, 2, 2), rt_half_sem.at[1], down_y)

    def act_opposite():
        got(r_blocks(opposite, 0, 2), rt_half_sem.at[0])
        got(r_blocks(opposite, 2, 2), rt_half_sem.at[1])

    def finish_sums():
        for i in range(8):
            got(x_in.at[i], x_send_sem.at[i])

    def finish_spreads(first, last):
        for i in range(first, last):
            got(grad.at[i, pl.ds(0, 96)], gx_send_sem.at[i])

    def finish_act():
        got(r_in, r_send_sem.at[0])
        for side in range(2):
            got(r_blocks(y, 0, 4), rt_y_send_sem.at[side])

    def opposite_pair(h):
        for k in range(2):
            got(half_shard(opposite, 2 * h + k, 0), a_half_sem.at[0, 2 * h + k])
            got(half_shard(opposite, 2 * h + k, 1), a_half_sem.at[1, 2 * h + k])

    mate = zl + 1 - 2 * (zl % 2)

    def relay_far():
        relay_shard_y(2 * far)
        relay_shard_y(2 * far + 1)

    stages = [rotate, sum_core, sum_x, sum_z, spread_core]

    def slot(s):
        for stage in reversed(range(len(stages))):
            if 0 <= s - stage < 8:
                stages[stage](s - stage)

    tokens_x()
    basis_relay()
    send_shard_y(zl, grads_ref)
    z_step(1)
    own_a.wait()
    own_basis.wait()
    rotate(0)
    sum_core(0)
    z_step(2)
    tokens_core()
    relay_shard_y(zl)
    sum_x(0)
    rotate_act()
    z_step(3)
    rotate(1)
    relay_shard_y(mate)
    sum_core(1)
    rotate(2)
    rotate(3)
    sum_core(2)
    sum_core(3)
    sum_z(0)
    sum_x(1)
    sum_act()
    relay_far()
    rotate(4)
    rotate(5)
    spread_core(0)
    sum_core(4)
    sum_core(5)
    sum_x(2)
    sum_z(1)
    sum_x(3)
    act_y(1)
    opposite_pair(near)
    rotate(6)
    act_y(2)
    act_y(3)
    sum_core(6)
    sum_z(2)
    sum_z(3)
    spread_core(1)
    sum_x(4)
    sum_x(5)
    opposite_pair(far)
    rotate(7)
    spread_core(2)
    spread_core(3)
    sum_core(7)
    act_relay()
    sum_z(4)
    sum_z(5)
    sum_x(6)
    fit(0)
    copies.finish(25)
    sum_x(7)
    sum_z(6)
    spread_core(4)
    spread_core(5)
    fit(1)
    finish_sums()
    sum_z(7)
    spread_core(6)
    fit(2)
    finish_spreads(0, 6)
    finish_act()
    spread_core(7)
    copies.finish(3)
    finish_spreads(6, 8)
    act_opposite()
    fit(3)
    copies.finish()


def call(arrays, r_type, collective_id):
    vmem = pl.BlockSpec(memory_space=pltpu.VMEM)
    dma = pltpu.SemaphoreType.DMA
    return pl.pallas_call(
        functools.partial(kernel, r_type),
        out_shape=jax.ShapeDtypeStruct((512, 896), F32),
        in_specs=[vmem] * 3 + [pl.BlockSpec(memory_space=pl.ANY)],
        out_specs=vmem,
        scratch_shapes=[
            pltpu.VMEM((2048, 1792), BF16),
            pltpu.VMEM((8, 256, 896), F32),
            pltpu.VMEM((8, 128, 896), F32),
            pltpu.VMEM((8, 3, 32, 896), F32),
            pltpu.VMEM((8, 32, 896), F32),
            pltpu.VMEM((8, 32, 896), F32),
            pltpu.VMEM((8, 256, 896), BF16),
            pltpu.VMEM((2048, 512), BF16),
            pltpu.VMEM((2, 4, 2, 128, 512), BF16),
            pltpu.VMEM((4, 128, 512), F32),
            pltpu.VMEM((4, 128, 512), BF16),
            pltpu.VMEM((3, 128, 512), r_type),
            pltpu.VMEM((16, 512, 128), BF16),
            pltpu.VMEM((1792, 896), BF16),
            dma((200,)),
            dma((4,)),
            dma((3, 4)),
            dma((2, 4)),
            dma((2,)),
            dma((2,)),
            dma((2, 2)),
            dma((4,)),
            dma((1,)),
            dma((1,)),
            dma((1,)),
            dma((3,)),
            dma((2,)),
            dma((2,)),
            dma((2,)),
            dma((8,)),
            dma((8,)),
            dma((8,)),
            dma((8,)),
            dma((8,)),
            dma((8,)),
            dma((8,)),
        ],
        compiler_params=pltpu.CompilerParams(
            collective_id=collective_id, has_side_effects=True, vmem_limit_bytes=56 * 2**20
        ),
        cost_estimate=pl.CostEstimate(flops=9_600_000_000, bytes_accessed=6_000_000, transcendentals=0),
    )(*arrays)


def solution(mesh):
    in_specs = (P("dp", "tensor"), P("dp", "tensor"), P("dp", "tensor"), P("tensor", "dp"))
    out_specs = P("tensor", "dp")

    def local(*arrays):
        return call(arrays, BF16, 0)

    return jax.shard_map(local, mesh=mesh, in_specs=in_specs, out_specs=out_specs, check_vma=False)
```

```python
import functools

import jax
import jax.numpy as jnp
from jax import lax
from jax.experimental import pallas as pl
from jax.experimental.pallas import tpu as pltpu
from jax.sharding import PartitionSpec as P

MESH = pl.DeviceIdType.MESH
F32 = jnp.float32
BF16 = jnp.bfloat16
SEQ = 128


class Copies:
    def __init__(self, send_sems):
        self.send_sems = send_sems
        self.sent = []
        self.count = 0

    def send(self, src, dst, recv_sem, to, cond=None, shared=None):
        index = self.count

        def build():
            return pltpu.make_async_remote_copy(
                src_ref=src,
                dst_ref=dst,
                send_sem=self.send_sems.at[index] if shared is None else shared,
                recv_sem=recv_sem,
                device_id=to,
                device_id_type=MESH,
            )

        if cond is None:
            build().start()
        else:
            pl.when(cond)(lambda: build().start())
        if shared is None:
            self.count += 1
            self.sent.append((build, cond))

    def finish(self, keep=0):
        done = self.sent[:len(self.sent) - keep]
        self.sent = self.sent[len(done):]
        for build, cond in done:
            if cond is None:
                build().wait_send()
            else:
                pl.when(cond)(lambda build=build: build().wait_send())


def kernel(
    r_type,
    tokens_ref, grads_ref, bin_ref, bout_hbm, out_ref,
    a_all, part, core_in, x_in, x_sum, z_in, grad, b1, a1, r_part, r_out, r_in, rt,
    bout_ref, send_sems, local_sems, a_sem, a_half_sem, b1_sem, b1_half_sem, a1_first_sem, a1_x_sem, a1_core_sem,
    r_sem, r_send_sem, rt_z_sem, rt_y_sem, rt_y_send_sem, rt_half_sem, core_sem, x_sem, x_send_sem, z_sem, gx_sem, gx_send_sem, gc_sem,
):
    dp, tensor = lax.axis_index("dp"), lax.axis_index("tensor")
    y, zl = dp // 4, dp % 4
    zh, x, c = tensor // 8, (tensor // 2) % 4, tensor % 2

    def dev(x=x, y=y, zl=zl, zh=zh, c=c):
        return (y * 4 + zl, zh * 8 + x * 2 + c)

    def ring(v, k):
        return lax.rem(v + k + 4, 4)

    up_y, down_y = dev(y=ring(y, 1)), dev(y=ring(y, -1))
    core_mate, z_mate = dev(c=1 - c), dev(zh=1 - zh)
    x_others = [dev(x=ring(x, k)) for k in (1, 2, 3)]
    copies = Copies(send_sems)

    own_basis = pltpu.make_async_copy(bout_hbm, bout_ref, local_sems.at[3])
    own_basis.start()

    barrier = pltpu.get_barrier_semaphore()
    greeted = 0
    for dz in range(4):
        for dh in range(2):
            for dc in range(2):
                if dz or dh or dc:
                    pl.semaphore_signal(
                        barrier, inc=1, device_id=dev(zl=ring(zl, dz), zh=(zh + dh) % 2, c=(c + dc) % 2), device_id_type=MESH
                    )
                    greeted += 1
    for other in [up_y, down_y] + x_others:
        pl.semaphore_signal(barrier, inc=1, device_id=other, device_id_type=MESH)
        greeted += 1
    pl.semaphore_wait(barrier, greeted)

    def got(ref, sem):
        pltpu.make_async_copy(ref, ref, sem).wait()

    def shard(yy, zz):
        return a_all.at[pl.ds(pl.multiple_of((yy * 4 + zz) * SEQ, SEQ), SEQ)]

    def half_shard(yy, zz, half):
        return a_all.at[pl.ds(pl.multiple_of((yy * 4 + zz) * SEQ + half * (SEQ // 2), SEQ // 2), SEQ // 2)]

    def send_shard_y(zz, src, cond=None):
        copies.send(src, shard(y, zz), a_sem.at[1, zz], up_y, cond)
        copies.send(src, shard(y, zz), a_sem.at[2, zz], down_y, cond)

    low, high, opposite = ring(y, -1), ring(y, 1), ring(y, 2)

    def relay_shard_y(zz):
        got(shard(low, zz), a_sem.at[1, zz])
        copies.send(half_shard(low, zz, 0), half_shard(low, zz, 0), a_half_sem.at[0, zz], up_y)
        got(shard(high, zz), a_sem.at[2, zz])
        copies.send(half_shard(high, zz, 1), half_shard(high, zz, 1), a_half_sem.at[1, zz], down_y)

    z_target = 2 * (x % 2) + c
    a1_block = a1.at[zl % 2, 2 * zh + x // 2, zl // 2]
    for h in range(2):
        mine = jnp.logical_and(zl == z_target, zh == h)
        copies.send(
            tokens_ref, a1_block, a1_first_sem.at[zl // 2, zh], dev(zl=z_target, zh=h, c=zl % 2), jnp.logical_not(mine)
        )

        @pl.when(mine)
        def _():
            own = pltpu.make_async_copy(tokens_ref, a1_block, local_sems.at[2])
            own.start()
            own.wait()

    def b1_block(yy):
        return b1.at[pl.ds(pl.multiple_of(yy * 512, 512), 512)]

    def b1_half(yy, half):
        return b1.at[pl.ds(pl.multiple_of(yy * 512 + half * 256, 256), 256)]

    copies.send(bin_ref, b1_block(y), b1_sem.at[0], up_y)
    copies.send(bin_ref, b1_block(y), b1_sem.at[1], down_y)
    copies.send(grads_ref, shard(y, zl), a_sem.at[0, zl], dev(zl=jnp.minimum(zl + 1, 3)), zl < 3)
    copies.send(grads_ref, shard(y, zl), a_sem.at[0, zl], dev(zl=jnp.maximum(zl - 1, 0)), zl > 0)

    own_a = pltpu.make_async_copy(grads_ref, shard(y, zl), local_sems.at[0])
    own_b = pltpu.make_async_copy(bin_ref, b1_block(y), local_sems.at[1])
    own_a.start()
    own_b.start()

    def z_step(k):
        for sign in (-1, 1):
            source = zl + sign * k
            there = jnp.logical_and(source >= 0, source <= 3)
            zz = jnp.clip(source, 0, 3)
            pl.when(there)(lambda zz=zz: got(shard(y, zz), a_sem.at[0, zz]))
            if k < 3:
                onward = zl - sign
                copies.send(
                    shard(y, zz), shard(y, zz), a_sem.at[0, zz], dev(zl=jnp.clip(onward, 0, 3)),
                    jnp.logical_and(there, jnp.logical_and(onward >= 0, onward <= 3)),
                )
            send_shard_y(zz, shard(y, zz), there)

    parity = zl // 2

    def tokens_x():
        holds = x % 2 == parity
        for zhalf in range(2):
            for h in range(2):
                mine = jnp.logical_and(c + 2 * zhalf == zl, zh == h)
                pl.when(jnp.logical_and(holds, jnp.logical_not(mine)))(
                    lambda zhalf=zhalf, h=h: got(a1.at[c, 2 * h + x // 2, zhalf], a1_first_sem.at[zhalf, h])
                )
        for h in range(2):
            block = a1.at[c, 2 * h + x // 2]
            for other in x_others:
                copies.send(block, block, a1_x_sem.at[2 * h + x // 2], other, holds)

    def tokens_core():
        for kq in range(4):
            pl.when(parity + 2 * (kq % 2) != x)(lambda kq=kq: got(a1.at[c, kq], a1_x_sem.at[kq]))
        copies.send(a1.at[c], a1.at[c], a1_core_sem.at[0], core_mate)

    def basis_relay():
        got(b1_block(low), b1_sem.at[0])
        copies.send(b1_half(low, 0), b1_half(low, 0), b1_half_sem.at[0], up_y)
        got(b1_block(high), b1_sem.at[1])
        copies.send(b1_half(high, 1), b1_half(high, 1), b1_half_sem.at[1], down_y)

    near, far = zl // 2, 1 - zl // 2
    units = [(y, near), (y, far), (high, near), (low, near), (high, far), (low, far), (opposite, near), (opposite, far)]

    def rotate(i):
        g, h = units[i]
        rows = pl.ds(pl.multiple_of(g * 512 + h * 256, 256), 256)
        part[i] = jnp.dot(a_all[rows, :], bout_ref[...], preferred_element_type=F32)
        theirs = part.at[i, pl.ds(pl.multiple_of((1 - c) * 128, 128), 128)]
        copies.send(theirs, core_in.at[i], core_sem.at[i], core_mate)

    def sum_core(i):
        got(core_in.at[i], core_sem.at[i])
        rows = pl.ds(pl.multiple_of(c * 128, 128), 128)
        chip = part[i, rows, :] + core_in[i]
        part[i, rows, :] = chip
        for k, other in zip((1, 2, 3), x_others):
            piece = part.at[i, pl.ds(pl.multiple_of(c * 128 + ring(x, k) * 32, 32), 32)]
            copies.send(piece, x_in.at[i, k - 1], x_sem.at[i], other, shared=x_send_sem.at[i])

    def sum_x(i):
        got(x_in.at[i], x_sem.at[i])
        rows = pl.ds(pl.multiple_of(c * 128 + x * 32, 32), 32)
        x_sum[i] = (part[i, rows, :] + x_in[i, 0]) + (x_in[i, 1] + x_in[i, 2])
        copies.send(x_sum.at[i], z_in.at[i], z_sem.at[i], z_mate)

    def grad_rows(i, first, count):
        return grad.at[i, pl.ds(pl.multiple_of(first, count), count)]

    def sum_z(i):
        got(z_in.at[i], z_sem.at[i])
        first = c * 128 + x * 32
        grad[i, pl.ds(pl.multiple_of(first, 32), 32), :] = (x_sum[i] + z_in[i]).astype(BF16)
        own = grad_rows(i, first, 32)
        for other in x_others:
            copies.send(own, own, gx_sem.at[i], other, shared=gx_send_sem.at[i])

    def spread_core(i):
        got(grad.at[i, pl.ds(0, 96)], gx_sem.at[i])
        own = grad_rows(i, c * 128, 128)
        copies.send(own, own, gc_sem.at[i], core_mate)

    def fit(pair):
        examples = []
        for i in (2 * pair, 2 * pair + 1):
            got(grad_rows(i, (1 - c) * 128, 128), gc_sem.at[i])
            g, h = units[i]
            examples += [(g * 4 + h * 2 + n, i, n * SEQ) for n in range(2)]

        def tile(cols):
            total = None
            for example, i, first in examples:
                right = grad[i, first:first + SEQ, cols]
                product = jnp.dot(rt[example], right, preferred_element_type=F32)
                square = product * product
                total = square if total is None else total + square
            total = total * (1.0 / 2048)
            out_ref[:, cols] = total if pair == 0 else out_ref[:, cols] + total

        @pl.loop(0, 3)
        def _(j):
            tile(pl.ds(pl.multiple_of(j * 256, 256), 256))

        tile(pl.ds(768, 128))

    def place(zz):
        return (zz % 2) * 2 + zz // 2

    def rotate_act():
        own_b.wait()
        got(b1_half(opposite, 0), b1_half_sem.at[0])
        got(b1_half(opposite, 1), b1_half_sem.at[1])
        got(a1.at[1 - c], a1_core_sem.at[0])

        @pl.loop(0, 4)
        def _(kq):
            left = a1[:, kq].reshape(512, 512)
            right = b1[pl.ds(pl.multiple_of(kq * 512, 512), 512), :]
            term = jnp.dot(left, right, preferred_element_type=F32)

            @pl.when(kq == 0)
            def _():
                r_part[...] = term.reshape(4, SEQ, 512)

            @pl.when(kq != 0)
            def _():
                r_part[...] += term.reshape(4, SEQ, 512)

        source = r_part
        if r_type != F32:
            r_out[...] = r_part[...].astype(r_type)
            source = r_out
        for k in (1, 2, 3):
            zz = ring(zl, k)
            copies.send(source.at[place(zz)], r_in.at[k - 1], r_sem.at[0], dev(zl=zz), shared=r_send_sem.at[0])

    def r_block(yy, zz):
        return rt.at[yy * 4 + zz]

    def r_blocks(yy, first, count):
        return rt.at[pl.ds(yy * 4 + first, count)]

    def send_r_y(zz):
        copies.send(r_block(y, zz), r_block(y, zz), rt_y_sem.at[0], up_y, shared=rt_y_send_sem.at[0])
        copies.send(r_block(y, zz), r_block(y, zz), rt_y_sem.at[1], down_y, shared=rt_y_send_sem.at[1])

    def sum_act():
        got(r_in, r_sem.at[0])
        others = [r_in[k].astype(F32) for k in range(3)]
        own_r = (r_part[place(zl)] + others[0]) + (others[1] + others[2])
        rt[y * 4 + zl] = own_r.T.astype(BF16)
        for k in (1, 2, 3):
            copies.send(r_block(y, zl), r_block(y, zl), rt_z_sem.at[k - 1], dev(zl=ring(zl, k)))
        send_r_y(zl)

    def act_y(k):
        zz = ring(zl, -k)
        got(r_block(y, zz), rt_z_sem.at[k - 1])
        send_r_y(zz)

    def act_relay():
        got(r_blocks(low, 0, 4), rt_y_sem.at[0])
        copies.send(r_blocks(low, 0, 2), r_blocks(low, 0, 2), rt_half_sem.at[0], up_y)
        got(r_blocks(high, 0, 4), rt_y_sem.at[1])
        copies.send(r_blocks(high, 2, 2), r_blocks(high, 2, 2), rt_half_sem.at[1], down_y)

    def act_opposite():
        got(r_blocks(opposite, 0, 2), rt_half_sem.at[0])
        got(r_blocks(opposite, 2, 2), rt_half_sem.at[1])

    def finish_sums():
        for i in range(8):
            got(x_in.at[i], x_send_sem.at[i])

    def finish_spreads(first, last):
        for i in range(first, last):
            got(grad.at[i, pl.ds(0, 96)], gx_send_sem.at[i])

    def finish_act():
        got(r_in, r_send_sem.at[0])
        for side in range(2):
            got(r_blocks(y, 0, 4), rt_y_send_sem.at[side])

    def opposite_pair(h):
        for k in range(2):
            got(half_shard(opposite, 2 * h + k, 0), a_half_sem.at[0, 2 * h + k])
            got(half_shard(opposite, 2 * h + k, 1), a_half_sem.at[1, 2 * h + k])

    mate = zl + 1 - 2 * (zl % 2)

    def relay_far():
        relay_shard_y(1 + far)
        relay_shard_y(3 * far)

    stages = [rotate, sum_core, sum_x, sum_z, spread_core]

    def slot(s):
        for stage in reversed(range(len(stages))):
            if 0 <= s - stage < 8:
                stages[stage](s - stage)

    tokens_x()
    basis_relay()
    send_shard_y(zl, grads_ref)
    z_step(1)
    own_a.wait()
    own_basis.wait()
    rotate(0)
    sum_core(0)
    z_step(2)
    tokens_core()
    relay_shard_y(zl)
    sum_x(0)
    rotate_act()
    z_step(3)
    rotate(1)
    relay_shard_y(mate)
    sum_core(1)
    rotate(2)
    rotate(3)
    sum_core(2)
    sum_core(3)
    sum_z(0)
    sum_x(1)
    sum_act()
    relay_far()
    rotate(4)
    rotate(5)
    spread_core(0)
    sum_core(4)
    sum_core(5)
    sum_x(2)
    sum_z(1)
    sum_x(3)
    act_y(1)
    opposite_pair(near)
    rotate(6)
    act_y(2)
    act_y(3)
    sum_core(6)
    sum_z(2)
    sum_z(3)
    spread_core(1)
    sum_x(4)
    sum_x(5)
    opposite_pair(far)
    rotate(7)
    spread_core(2)
    spread_core(3)
    sum_core(7)
    act_relay()
    sum_z(4)
    sum_z(5)
    sum_x(6)
    fit(0)
    copies.finish(25)
    sum_x(7)
    sum_z(6)
    spread_core(4)
    spread_core(5)
    fit(1)
    finish_sums()
    sum_z(7)
    spread_core(6)
    fit(2)
    finish_spreads(0, 6)
    finish_act()
    spread_core(7)
    copies.finish(3)
    finish_spreads(6, 8)
    act_opposite()
    fit(3)
    copies.finish()


def call(arrays, r_type, collective_id):
    vmem = pl.BlockSpec(memory_space=pltpu.VMEM)
    dma = pltpu.SemaphoreType.DMA
    return pl.pallas_call(
        functools.partial(kernel, r_type),
        out_shape=jax.ShapeDtypeStruct((512, 896), F32),
        in_specs=[vmem] * 3 + [pl.BlockSpec(memory_space=pl.ANY)],
        out_specs=vmem,
        scratch_shapes=[
            pltpu.VMEM((2048, 1792), BF16),
            pltpu.VMEM((8, 256, 896), F32),
            pltpu.VMEM((8, 128, 896), F32),
            pltpu.VMEM((8, 3, 32, 896), F32),
            pltpu.VMEM((8, 32, 896), F32),
            pltpu.VMEM((8, 32, 896), F32),
            pltpu.VMEM((8, 256, 896), BF16),
            pltpu.VMEM((2048, 512), BF16),
            pltpu.VMEM((2, 4, 2, 128, 512), BF16),
            pltpu.VMEM((4, 128, 512), F32),
            pltpu.VMEM((4, 128, 512), BF16),
            pltpu.VMEM((3, 128, 512), r_type),
            pltpu.VMEM((16, 512, 128), BF16),
            pltpu.VMEM((1792, 896), BF16),
            dma((200,)),
            dma((4,)),
            dma((3, 4)),
            dma((2, 4)),
            dma((2,)),
            dma((2,)),
            dma((2, 2)),
            dma((4,)),
            dma((1,)),
            dma((1,)),
            dma((1,)),
            dma((3,)),
            dma((2,)),
            dma((2,)),
            dma((2,)),
            dma((8,)),
            dma((8,)),
            dma((8,)),
            dma((8,)),
            dma((8,)),
            dma((8,)),
            dma((8,)),
        ],
        compiler_params=pltpu.CompilerParams(
            collective_id=collective_id, has_side_effects=True, vmem_limit_bytes=56 * 2**20
        ),
        cost_estimate=pl.CostEstimate(flops=9_600_000_000, bytes_accessed=6_000_000, transcendentals=0),
    )(*arrays)


def solution(mesh):
    in_specs = (P("dp", "tensor"), P("dp", "tensor"), P("dp", "tensor"), P("tensor", "dp"))
    out_specs = P("tensor", "dp")

    def local(*arrays):
        return call(arrays, BF16, 0)

    return jax.shard_map(local, mesh=mesh, in_specs=in_specs, out_specs=out_specs, check_vma=False)
```

```python
import functools

import jax
import jax.numpy as jnp
from jax import lax
from jax.experimental import pallas as pl
from jax.experimental.pallas import tpu as pltpu
from jax.sharding import PartitionSpec as P

MESH = pl.DeviceIdType.MESH
F32 = jnp.float32
BF16 = jnp.bfloat16
SEQ = 128


class Copies:
    def __init__(self, send_sems):
        self.send_sems = send_sems
        self.sent = []
        self.count = 0

    def send(self, src, dst, recv_sem, to, cond=None, shared=None):
        index = self.count

        def build():
            return pltpu.make_async_remote_copy(
                src_ref=src,
                dst_ref=dst,
                send_sem=self.send_sems.at[index] if shared is None else shared,
                recv_sem=recv_sem,
                device_id=to,
                device_id_type=MESH,
            )

        if cond is None:
            build().start()
        else:
            pl.when(cond)(lambda: build().start())
        if shared is None:
            self.count += 1
            self.sent.append((build, cond))

    def finish(self, keep=0):
        done = self.sent[:len(self.sent) - keep]
        self.sent = self.sent[len(done):]
        for build, cond in done:
            if cond is None:
                build().wait_send()
            else:
                pl.when(cond)(lambda build=build: build().wait_send())


def kernel(
    r_type,
    tokens_ref, grads_ref, bin_ref, bout_hbm, out_ref,
    a_all, part, core_in, x_in, x_sum, z_in, grad, b1, a1, r_part, r_out, r_in, rt,
    bout_ref, send_sems, local_sems, a_sem, a_half_sem, b1_sem, b1_half_sem, a1_first_sem, a1_x_sem, a1_core_sem,
    r_sem, r_send_sem, rt_z_sem, rt_y_sem, rt_y_send_sem, rt_half_sem, core_sem, x_sem, x_send_sem, z_sem, gx_sem, gx_send_sem, gc_sem,
):
    dp, tensor = lax.axis_index("dp"), lax.axis_index("tensor")
    y, zl = dp // 4, dp % 4
    zh, x, c = tensor // 8, (tensor // 2) % 4, tensor % 2

    def dev(x=x, y=y, zl=zl, zh=zh, c=c):
        return (y * 4 + zl, zh * 8 + x * 2 + c)

    def ring(v, k):
        return lax.rem(v + k + 4, 4)

    up_y, down_y = dev(y=ring(y, 1)), dev(y=ring(y, -1))
    core_mate, z_mate = dev(c=1 - c), dev(zh=1 - zh)
    x_others = [dev(x=ring(x, k)) for k in (1, 2, 3)]
    copies = Copies(send_sems)

    own_basis = pltpu.make_async_copy(bout_hbm, bout_ref, local_sems.at[3])
    own_basis.start()

    barrier = pltpu.get_barrier_semaphore()
    greeted = 0
    for dz in range(4):
        for dh in range(2):
            for dc in range(2):
                if dz or dh or dc:
                    pl.semaphore_signal(
                        barrier, inc=1, device_id=dev(zl=ring(zl, dz), zh=(zh + dh) % 2, c=(c + dc) % 2), device_id_type=MESH
                    )
                    greeted += 1
    for other in [up_y, down_y] + x_others:
        pl.semaphore_signal(barrier, inc=1, device_id=other, device_id_type=MESH)
        greeted += 1
    pl.semaphore_wait(barrier, greeted)

    def got(ref, sem):
        pltpu.make_async_copy(ref, ref, sem).wait()

    def shard(yy, zz):
        return a_all.at[pl.ds(pl.multiple_of((yy * 4 + zz) * SEQ, SEQ), SEQ)]

    def half_shard(yy, zz, half):
        return a_all.at[pl.ds(pl.multiple_of((yy * 4 + zz) * SEQ + half * (SEQ // 2), SEQ // 2), SEQ // 2)]

    def send_shard_y(zz, src, cond=None):
        copies.send(src, shard(y, zz), a_sem.at[1, zz], up_y, cond)
        copies.send(src, shard(y, zz), a_sem.at[2, zz], down_y, cond)

    low, high, opposite = ring(y, -1), ring(y, 1), ring(y, 2)

    def relay_shard_y(zz):
        got(shard(low, zz), a_sem.at[1, zz])
        copies.send(half_shard(low, zz, 0), half_shard(low, zz, 0), a_half_sem.at[0, zz], up_y)
        got(shard(high, zz), a_sem.at[2, zz])
        copies.send(half_shard(high, zz, 1), half_shard(high, zz, 1), a_half_sem.at[1, zz], down_y)

    z_target = 2 * (x % 2) + c
    a1_block = a1.at[zl % 2, 2 * zh + x // 2, zl // 2]
    for h in range(2):
        mine = jnp.logical_and(zl == z_target, zh == h)
        copies.send(
            tokens_ref, a1_block, a1_first_sem.at[zl // 2, zh], dev(zl=z_target, zh=h, c=zl % 2), jnp.logical_not(mine)
        )

        @pl.when(mine)
        def _():
            own = pltpu.make_async_copy(tokens_ref, a1_block, local_sems.at[2])
            own.start()
            own.wait()

    def b1_block(yy):
        return b1.at[pl.ds(pl.multiple_of(yy * 512, 512), 512)]

    def b1_half(yy, half):
        return b1.at[pl.ds(pl.multiple_of(yy * 512 + half * 256, 256), 256)]

    copies.send(bin_ref, b1_block(y), b1_sem.at[0], up_y)
    copies.send(bin_ref, b1_block(y), b1_sem.at[1], down_y)
    copies.send(grads_ref, shard(y, zl), a_sem.at[0, zl], dev(zl=jnp.minimum(zl + 1, 3)), zl < 3)
    copies.send(grads_ref, shard(y, zl), a_sem.at[0, zl], dev(zl=jnp.maximum(zl - 1, 0)), zl > 0)

    own_a = pltpu.make_async_copy(grads_ref, shard(y, zl), local_sems.at[0])
    own_b = pltpu.make_async_copy(bin_ref, b1_block(y), local_sems.at[1])
    own_a.start()
    own_b.start()

    def z_step(k):
        for sign in (-1, 1):
            source = zl + sign * k
            there = jnp.logical_and(source >= 0, source <= 3)
            zz = jnp.clip(source, 0, 3)
            pl.when(there)(lambda zz=zz: got(shard(y, zz), a_sem.at[0, zz]))
            if k < 3:
                onward = zl - sign
                copies.send(
                    shard(y, zz), shard(y, zz), a_sem.at[0, zz], dev(zl=jnp.clip(onward, 0, 3)),
                    jnp.logical_and(there, jnp.logical_and(onward >= 0, onward <= 3)),
                )
            send_shard_y(zz, shard(y, zz), there)

    parity = zl // 2

    def tokens_x():
        holds = x % 2 == parity
        for zhalf in range(2):
            for h in range(2):
                mine = jnp.logical_and(c + 2 * zhalf == zl, zh == h)
                pl.when(jnp.logical_and(holds, jnp.logical_not(mine)))(
                    lambda zhalf=zhalf, h=h: got(a1.at[c, 2 * h + x // 2, zhalf], a1_first_sem.at[zhalf, h])
                )
        for h in range(2):
            block = a1.at[c, 2 * h + x // 2]
            for other in x_others:
                copies.send(block, block, a1_x_sem.at[2 * h + x // 2], other, holds)

    def tokens_core():
        for kq in range(4):
            pl.when(parity + 2 * (kq % 2) != x)(lambda kq=kq: got(a1.at[c, kq], a1_x_sem.at[kq]))
        copies.send(a1.at[c], a1.at[c], a1_core_sem.at[0], core_mate)

    def basis_relay():
        got(b1_block(low), b1_sem.at[0])
        copies.send(b1_half(low, 0), b1_half(low, 0), b1_half_sem.at[0], up_y)
        got(b1_block(high), b1_sem.at[1])
        copies.send(b1_half(high, 1), b1_half(high, 1), b1_half_sem.at[1], down_y)

    near, far = zl // 2, 1 - zl // 2
    units = [(y, near), (y, far), (high, near), (low, near), (high, far), (low, far), (opposite, near), (opposite, far)]

    def rotate(i):
        g, h = units[i]
        rows = pl.ds(pl.multiple_of(g * 512 + h * 256, 256), 256)
        part[i] = jnp.dot(a_all[rows, :], bout_ref[...], preferred_element_type=F32)
        theirs = part.at[i, pl.ds(pl.multiple_of((1 - c) * 128, 128), 128)]
        copies.send(theirs, core_in.at[i], core_sem.at[i], core_mate)

    def sum_core(i):
        got(core_in.at[i], core_sem.at[i])
        rows = pl.ds(pl.multiple_of(c * 128, 128), 128)
        chip = part[i, rows, :] + core_in[i]
        part[i, rows, :] = chip
        for k, other in zip((1, 2, 3), x_others):
            piece = part.at[i, pl.ds(pl.multiple_of(c * 128 + ring(x, k) * 32, 32), 32)]
            copies.send(piece, x_in.at[i, k - 1], x_sem.at[i], other, shared=x_send_sem.at[i])

    def sum_x(i):
        got(x_in.at[i], x_sem.at[i])
        rows = pl.ds(pl.multiple_of(c * 128 + x * 32, 32), 32)
        x_sum[i] = (part[i, rows, :] + x_in[i, 0]) + (x_in[i, 1] + x_in[i, 2])
        copies.send(x_sum.at[i], z_in.at[i], z_sem.at[i], z_mate)

    def grad_rows(i, first, count):
        return grad.at[i, pl.ds(pl.multiple_of(first, count), count)]

    def sum_z(i):
        got(z_in.at[i], z_sem.at[i])
        first = c * 128 + x * 32
        grad[i, pl.ds(pl.multiple_of(first, 32), 32), :] = (x_sum[i] + z_in[i]).astype(BF16)
        own = grad_rows(i, first, 32)
        for other in x_others:
            copies.send(own, own, gx_sem.at[i], other, shared=gx_send_sem.at[i])

    def spread_core(i):
        got(grad.at[i, pl.ds(0, 96)], gx_sem.at[i])
        own = grad_rows(i, c * 128, 128)
        copies.send(own, own, gc_sem.at[i], core_mate)

    def fit(pair):
        examples = []
        for i in (2 * pair, 2 * pair + 1):
            got(grad_rows(i, (1 - c) * 128, 128), gc_sem.at[i])
            g, h = units[i]
            examples += [(g * 4 + h * 2 + n, i, n * SEQ) for n in range(2)]

        def tile(cols):
            total = None
            for example, i, first in examples:
                right = grad[i, first:first + SEQ, cols]
                product = jnp.dot(rt[example], right, preferred_element_type=F32)
                square = product * product
                total = square if total is None else total + square
            total = total * (1.0 / 2048)
            out_ref[:, cols] = total if pair == 0 else out_ref[:, cols] + total

        @pl.loop(0, 3)
        def _(j):
            tile(pl.ds(pl.multiple_of(j * 256, 256), 256))

        tile(pl.ds(768, 128))

    def mirror(v):
        return jnp.where(zl < 2, v, 3 - v)

    last = mirror(1 - jnp.minimum(zl, 3 - zl))
    far_first = [mirror(3), mirror(2), last]
    arrivals = [mirror(2), mirror(3), last]

    def gap(source, target):
        return lax.rem(target - source + 4, 4) - 1

    def place(zz):
        return (zz % 2) * 2 + zz // 2

    def rotate_act():
        own_b.wait()
        got(b1_half(opposite, 0), b1_half_sem.at[0])
        got(b1_half(opposite, 1), b1_half_sem.at[1])
        got(a1.at[1 - c], a1_core_sem.at[0])

        @pl.loop(0, 4)
        def _(kq):
            left = a1[:, kq].reshape(512, 512)
            right = b1[pl.ds(pl.multiple_of(kq * 512, 512), 512), :]
            term = jnp.dot(left, right, preferred_element_type=F32)

            @pl.when(kq == 0)
            def _():
                r_part[...] = term.reshape(4, SEQ, 512)

            @pl.when(kq != 0)
            def _():
                r_part[...] += term.reshape(4, SEQ, 512)

        source = r_part
        if r_type != F32:
            r_out[...] = r_part[...].astype(r_type)
            source = r_out
        for zz in far_first:
            copies.send(source.at[place(zz)], r_in.at[gap(zl, zz)], r_sem.at[0], dev(zl=zz), shared=r_send_sem.at[0])

    def r_block(yy, zz):
        return rt.at[yy * 4 + zz]

    def r_blocks(yy, first, count):
        return rt.at[pl.ds(yy * 4 + first, count)]

    def send_r_y(zz):
        copies.send(r_block(y, zz), r_block(y, zz), rt_y_sem.at[0], up_y, shared=rt_y_send_sem.at[0])
        copies.send(r_block(y, zz), r_block(y, zz), rt_y_sem.at[1], down_y, shared=rt_y_send_sem.at[1])

    def sum_act():
        got(r_in, r_sem.at[0])
        others = [r_in[k].astype(F32) for k in range(3)]
        own_r = (r_part[place(zl)] + others[0]) + (others[1] + others[2])
        rt[y * 4 + zl] = own_r.T.astype(BF16)
        for zz in far_first:
            copies.send(r_block(y, zl), r_block(y, zl), rt_z_sem.at[gap(zl, zz)], dev(zl=zz))
        send_r_y(zl)

    def act_y(k):
        zz = arrivals[k - 1]
        got(r_block(y, zz), rt_z_sem.at[gap(zz, zl)])
        send_r_y(zz)

    def act_relay():
        got(r_blocks(low, 0, 4), rt_y_sem.at[0])
        copies.send(r_blocks(low, 0, 2), r_blocks(low, 0, 2), rt_half_sem.at[0], up_y)
        got(r_blocks(high, 0, 4), rt_y_sem.at[1])
        copies.send(r_blocks(high, 2, 2), r_blocks(high, 2, 2), rt_half_sem.at[1], down_y)

    def act_opposite():
        got(r_blocks(opposite, 0, 2), rt_half_sem.at[0])
        got(r_blocks(opposite, 2, 2), rt_half_sem.at[1])

    def finish_sums():
        for i in range(8):
            got(x_in.at[i], x_send_sem.at[i])

    def finish_spreads(first, last):
        for i in range(first, last):
            got(grad.at[i, pl.ds(0, 96)], gx_send_sem.at[i])

    def finish_act():
        got(r_in, r_send_sem.at[0])
        for side in range(2):
            got(r_blocks(y, 0, 4), rt_y_send_sem.at[side])

    def opposite_pair(h):
        for k in range(2):
            got(half_shard(opposite, 2 * h + k, 0), a_half_sem.at[0, 2 * h + k])
            got(half_shard(opposite, 2 * h + k, 1), a_half_sem.at[1, 2 * h + k])

    mate = zl + 1 - 2 * (zl % 2)

    def relay_far():
        relay_shard_y(1 + far)
        relay_shard_y(3 * far)

    stages = [rotate, sum_core, sum_x, sum_z, spread_core]

    def slot(s):
        for stage in reversed(range(len(stages))):
            if 0 <= s - stage < 8:
                stages[stage](s - stage)

    tokens_x()
    basis_relay()
    send_shard_y(zl, grads_ref)
    z_step(1)
    own_a.wait()
    own_basis.wait()
    rotate(0)
    sum_core(0)
    z_step(2)
    tokens_core()
    relay_shard_y(zl)
    sum_x(0)
    rotate_act()
    z_step(3)
    rotate(1)
    relay_shard_y(mate)
    sum_core(1)
    rotate(2)
    rotate(3)
    sum_core(2)
    sum_core(3)
    sum_z(0)
    sum_x(1)
    sum_act()
    relay_far()
    rotate(4)
    rotate(5)
    spread_core(0)
    sum_core(4)
    sum_core(5)
    sum_x(2)
    sum_z(1)
    sum_x(3)
    act_y(1)
    opposite_pair(near)
    rotate(6)
    act_y(2)
    act_y(3)
    sum_core(6)
    sum_z(2)
    sum_z(3)
    spread_core(1)
    sum_x(4)
    sum_x(5)
    opposite_pair(far)
    rotate(7)
    spread_core(2)
    spread_core(3)
    sum_core(7)
    act_relay()
    sum_z(4)
    sum_z(5)
    sum_x(6)
    fit(0)
    copies.finish(25)
    sum_x(7)
    sum_z(6)
    spread_core(4)
    spread_core(5)
    fit(1)
    finish_sums()
    sum_z(7)
    spread_core(6)
    fit(2)
    finish_spreads(0, 6)
    finish_act()
    spread_core(7)
    copies.finish(3)
    finish_spreads(6, 8)
    act_opposite()
    fit(3)
    copies.finish()


def call(arrays, r_type, collective_id):
    vmem = pl.BlockSpec(memory_space=pltpu.VMEM)
    dma = pltpu.SemaphoreType.DMA
    return pl.pallas_call(
        functools.partial(kernel, r_type),
        out_shape=jax.ShapeDtypeStruct((512, 896), F32),
        in_specs=[vmem] * 3 + [pl.BlockSpec(memory_space=pl.ANY)],
        out_specs=vmem,
        scratch_shapes=[
            pltpu.VMEM((2048, 1792), BF16),
            pltpu.VMEM((8, 256, 896), F32),
            pltpu.VMEM((8, 128, 896), F32),
            pltpu.VMEM((8, 3, 32, 896), F32),
            pltpu.VMEM((8, 32, 896), F32),
            pltpu.VMEM((8, 32, 896), F32),
            pltpu.VMEM((8, 256, 896), BF16),
            pltpu.VMEM((2048, 512), BF16),
            pltpu.VMEM((2, 4, 2, 128, 512), BF16),
            pltpu.VMEM((4, 128, 512), F32),
            pltpu.VMEM((4, 128, 512), BF16),
            pltpu.VMEM((3, 128, 512), r_type),
            pltpu.VMEM((16, 512, 128), BF16),
            pltpu.VMEM((1792, 896), BF16),
            dma((200,)),
            dma((4,)),
            dma((3, 4)),
            dma((2, 4)),
            dma((2,)),
            dma((2,)),
            dma((2, 2)),
            dma((4,)),
            dma((1,)),
            dma((1,)),
            dma((1,)),
            dma((3,)),
            dma((2,)),
            dma((2,)),
            dma((2,)),
            dma((8,)),
            dma((8,)),
            dma((8,)),
            dma((8,)),
            dma((8,)),
            dma((8,)),
            dma((8,)),
        ],
        compiler_params=pltpu.CompilerParams(
            collective_id=collective_id, has_side_effects=True, vmem_limit_bytes=56 * 2**20
        ),
        cost_estimate=pl.CostEstimate(flops=9_600_000_000, bytes_accessed=6_000_000, transcendentals=0),
    )(*arrays)


def solution(mesh):
    in_specs = (P("dp", "tensor"), P("dp", "tensor"), P("dp", "tensor"), P("tensor", "dp"))
    out_specs = P("tensor", "dp")

    def local(*arrays):
        return call(arrays, BF16, 0)

    return jax.shard_map(local, mesh=mesh, in_specs=in_specs, out_specs=out_specs, check_vma=False)
```
